32 devices in a mesh: grp: 8 (over z, y), shell: 4 (over x, core).
Axes of the slice: x: 2, y: 2, z: 4, core: 2. Of those that a mesh axis runs over, the one named last changes fastest.
Arguments:
- vectors: bfloat16 [8, 4, 384, 256], P('grp', 'shell'), may hold values from -6 to 6
- local_block: bfloat16 [8, 4, 384, 384], P('grp', 'shell'), may hold values from -0.3125 to 0.3125
- pair_blocks: bfloat16 [8, 4, 3, 384, 384], P('grp', 'shell'), may hold values from -0.3125 to 0.3125
- pair_masks: int32 [8, 4, 3, 3, 3], P('grp', 'shell'), may hold values 0 or 1
- shell_block: bfloat16 [8, 4, 384, 384], P('grp', 'shell'), may hold values from -0.3125 to 0.3125
- shell_mask: int32 [8, 4, 3, 3], P('grp', 'shell'), may hold values 0 or 1
- matchings: int32 [3, 8], replicated, may hold values from 0 to 7, as said below
Outputs:
- filtered: bfloat16 [8, 4, 384, 256], P('grp', 'shell')
The draws below stay inside these ranges and needn't reach their ends.
Inputs may be any that keep to these rules, and one draw needn't show every extreme that they name: Row m of matchings maps every group g to g XOR 2**b_m, for 3 distinct binary digits b_m drawn from the seed.
All inputs are finite; a program needn't handle non-finite values. No bound on the sum of `pair_masks` or of `shell_mask` on one device may be relied on, other than what follows from the above.
Results may differ from the reference program's by a relative error of at most 0.0049.
Values may be sent and summed in bfloat16 or wider, within the bound.
A program may use at most 64 MiB of HBM per device.

```python
import jax
import jax.numpy as jnp
from jax import lax

R = 384
NV = 256
DEG = 2
BLK = 128
RB = 3
MATCH = 3
N_GRP = 8
N_SHELL = 4


def draw_matchings(key, part):
    digits = N_GRP.bit_length() - 1
    own_key = jax.random.fold_in(key, 7919)
    scores = jax.random.randint(own_key, (digits,), 0, 1000003, dtype=jnp.int32)
    distinct = scores * digits + jnp.arange(digits, dtype=jnp.int32)
    order = jnp.argsort(distinct, stable=True).astype(jnp.int32)
    chosen_bits = order[:MATCH].astype(jnp.int32)
    groups = jnp.arange(N_GRP, dtype=jnp.int32)
    flips = jnp.left_shift(jnp.int32(1), chosen_bits)
    return jnp.bitwise_xor(groups[None, :], flips[:, None]).astype(jnp.int32)


def place_ends(values, key, low, high):
    extent = values.shape
    place = [jax.random.randint(jax.random.fold_in(key, axis), (), 0, extent[axis]) for axis in range(len(extent))]
    values = values.at[tuple(place)].set(low)
    longest = extent.index(max(extent))
    place[longest] = (place[longest] + 1) % extent[longest]
    return values.at[tuple(place)].set(high)


def block_scale(rng, extent, split, smallest, high):
    level, own = 1.0, jax.random.fold_in(rng, 6)
    for axis_at, shards_of in split:
        draws = jnp.exp(jax.random.uniform(jax.random.fold_in(own, axis_at), (shards_of,), jnp.float32, smallest / len(split), high / len(split)))
        level = level * jnp.repeat(draws, extent[axis_at] // shards_of).reshape([-1 if axis == axis_at else 1 for axis in range(len(extent))])
    return level


def centred(rng, extent, width, reach, pieces=(), held_as=jnp.bfloat16):
    values = width * jax.random.normal(rng, extent, jnp.float32)
    if pieces:
        values = values * block_scale(rng, extent, pieces, -0.22, 0.18)
    return jnp.clip(values, -reach, reach).astype(held_as)


def setup_inputs(seed: int = 0) -> dict:
    splits = jax.random.split(jax.random.key(seed), 8)
    return {
        "vectors": centred(splits[0], (N_GRP, N_SHELL, R, NV), 1.0, 6.0, ((0, 8), (1, 4))),
        "local_block": centred(splits[1], (N_GRP, N_SHELL, R, R), R ** -0.5, 0.3125, ((0, 8), (1, 4))),
        "pair_blocks": centred(splits[2], (N_GRP, N_SHELL, MATCH, R, R), R ** -0.5, 0.3125, ((0, 8), (1, 4))),
        "pair_masks": place_ends((jax.random.randint(splits[3], (N_GRP, N_SHELL, MATCH, RB, RB), 0, 4) < 3).astype(jnp.int32), jax.random.fold_in(splits[3], 1), 0, 1),
        "shell_block": centred(splits[4], (N_GRP, N_SHELL, R, R), R ** -0.5, 0.3125, ((0, 8), (1, 4))),
        "shell_mask": place_ends((jax.random.randint(splits[5], (N_GRP, N_SHELL, RB, RB), 0, 4) < 3).astype(jnp.int32), jax.random.fold_in(splits[5], 1), 0, 1),
        "matchings": draw_matchings(jax.random.fold_in(splits[7], 71), 0),
    }


spectrum_center = 1.0
spectrum_halfwidth = 6.0


def widen(mask):
    spread = jnp.repeat(jnp.repeat(mask, BLK, axis=-2), BLK, axis=-1)
    return spread.astype(jnp.bfloat16)


def apply_operator(vectors, local_block, pair_blocks, pair_masks, shell_block, shell_mask, matchings):
    groups = jnp.arange(N_GRP, dtype=jnp.int32)

    def partials(group):
        coupled_rows = (pair_blocks[group] * widen(pair_masks[group])).astype(jnp.float32)
        higher_rows = (shell_block[group] * widen(shell_mask[group])).astype(jnp.float32)
        resident_rows = vectors[group].astype(jnp.float32)
        returned = jnp.einsum("smrk,srv->smkv", coupled_rows, resident_rows).astype(jnp.bfloat16)
        lower_partner = jnp.einsum("yol,yox->ylx", higher_rows, resident_rows).astype(jnp.bfloat16)
        return returned, lower_partner

    returned, lower_partner = lax.map(partials, groups)

    def rows(group):
        coupled_rows = (pair_blocks[group] * widen(pair_masks[group])).astype(jnp.float32)
        higher_rows = (shell_block[group] * widen(shell_mask[group])).astype(jnp.float32)
        owned_rows = local_block[group].astype(jnp.float32)
        resident_rows = vectors[group].astype(jnp.float32)
        accumulated_rows = jnp.einsum("tjb,tbu->tju", owned_rows, resident_rows) + jnp.einsum("oqp,oqx->opx", owned_rows, resident_rows)
        for pairing_index in range(MATCH):
            partner = matchings[pairing_index, group]
            remote_rows = vectors[partner].astype(jnp.float32)
            accumulated_rows = accumulated_rows + jnp.einsum("tjb,tbu->tju", coupled_rows[:, pairing_index], remote_rows)
            accumulated_rows = accumulated_rows + returned[partner][:, pairing_index].astype(jnp.float32)
        zero_shell = jnp.zeros((1, R, NV), jnp.float32)
        higher_partner = jnp.concatenate([resident_rows[1:], zero_shell], axis=0)
        accumulated_rows = accumulated_rows + jnp.einsum("tjb,tbu->tju", higher_rows, higher_partner)
        lower_terms = lower_partner[group].astype(jnp.float32)
        accumulated_rows = accumulated_rows + jnp.concatenate([zero_shell, lower_terms[:-1]], axis=0)
        return accumulated_rows

    return lax.map(rows, groups)


def reference(vectors, local_block, pair_blocks, pair_masks, shell_block, shell_mask, matchings):
    def operate(current):
        return apply_operator(current, local_block, pair_blocks, pair_masks, shell_block, shell_mask, matchings)

    previous = vectors
    current = ((operate(vectors) - spectrum_center * vectors.astype(jnp.float32)) / spectrum_halfwidth).astype(jnp.bfloat16)
    for degree_step in range(1, DEG):
        image = operate(current)
        following = 2.0 * (image - spectrum_center * current.astype(jnp.float32)) / spectrum_halfwidth - previous.astype(jnp.float32)
        previous = current
        current = following.astype(jnp.bfloat16)
    return current
```

```python
import functools

import jax
import jax.numpy as jnp
from jax import lax
from jax.experimental import pallas as pl
from jax.experimental.pallas import tpu as pltpu
from jax.sharding import PartitionSpec as P

BLK = 128
LANES = 128

spectrum_center = 1.0
spectrum_halfwidth = 6.0

MESH = pl.DeviceIdType.MESH
F32 = jnp.float32
BF16 = jnp.bfloat16


def mm(a, b):
    return jnp.dot(a, b, preferred_element_type=F32)


def turned(x):
    return x.astype(F32).T


def filter_kernel(
    bits,
    shells,
    vec_hbm,
    local_hbm,
    pair_hbm,
    shell_hbm,
    pair_mask,
    shell_mask,
    matchings,
    out_hbm,
    vec,
    local_raw,
    pair_raw,
    shell_raw,
    own,
    theirs,
    full,
    full_t,
    sym,
    up,
    up_t,
    reply,
    arrived,
    lift,
    from_up,
    from_down,
    acc,
    result,
    load_sem,
    out_sem,
    block_send,
    block_recv,
    edge_send,
    edge_recv,
    down_send,
    down_recv,
    rise_send,
    rise_recv,
):
    halves = vec.shape[1]
    rows = vec.shape[2]
    parts = rows // BLK
    matches = pair_raw.shape[0]
    group = lax.axis_index("grp")
    shell = lax.axis_index("shell")
    has_up = shell < shells - 1
    has_down = shell > 0
    order = list(reversed(range(bits)))

    def digit(b):
        return (group // (1 << b)) % 2

    partner = [group + (1 << b) - 2 * (1 << b) * digit(b) for b in range(bits)]
    role = [(digit(b) + (digit((b + 1) % bits) if bits > 1 else 0) + shell) % 2 for b in range(bits)]
    holds = [role[b] == 1 for b in range(bits)]
    gives = [role[b] == 0 for b in range(bits)]

    columns = lambda h: pl.ds(h * LANES, LANES)
    loads = [pltpu.make_async_copy(pair_hbm, pair_raw, load_sem.at[0])]
    for h in range(halves):
        loads.append(pltpu.make_async_copy(vec_hbm.at[:, columns(h)], vec.at[0, h], load_sem.at[1 + h]))
    loads.append(pltpu.make_async_copy(shell_hbm, shell_raw, load_sem.at[1 + halves]))
    loads.append(pltpu.make_async_copy(local_hbm, local_raw, load_sem.at[2 + halves]))
    for load in loads:
        load.start()

    def block_copy(b):
        return pltpu.make_async_remote_copy(
            src_ref=own.at[b], dst_ref=theirs.at[b], send_sem=block_send.at[b], recv_sem=block_recv.at[b],
            device_id={"grp": partner[b]}, device_id_type=MESH)

    def edge_copy(source, step, b, h):
        return pltpu.make_async_remote_copy(
            src_ref=source, dst_ref=arrived.at[step, b, h], send_sem=edge_send.at[step, b, h],
            recv_sem=edge_recv.at[step, b, h], device_id={"grp": partner[b]}, device_id_type=MESH)

    def given_copy(step, b, h):
        return edge_copy(vec.at[step, h], step, b, h)

    def reply_copy(step, b, h):
        return edge_copy(reply.at[step, b, h], step, b, h)

    def down_copy(step, h):
        return pltpu.make_async_remote_copy(
            src_ref=vec.at[step, h], dst_ref=from_up.at[step, h], send_sem=down_send.at[step, h],
            recv_sem=down_recv.at[step, h], device_id={"shell": shell - 1}, device_id_type=MESH)

    def rise_copy(step, h):
        return pltpu.make_async_remote_copy(
            src_ref=lift.at[step, h], dst_ref=from_down.at[step, h], send_sem=rise_send.at[step, h],
            recv_sem=rise_recv.at[step, h], device_id={"shell": shell + 1}, device_id_type=MESH)

    barrier = pltpu.get_barrier_semaphore()
    for b in range(bits):
        pl.semaphore_signal(barrier, inc=1, device_id={"grp": partner[b]}, device_id_type=MESH)

    @pl.when(has_up)
    def _():
        pl.semaphore_signal(barrier, inc=1, device_id={"shell": shell + 1}, device_id_type=MESH)

    @pl.when(has_down)
    def _():
        pl.semaphore_signal(barrier, inc=1, device_id={"shell": shell - 1}, device_id_type=MESH)

    neighbours = bits + jnp.where(has_up, 1, 0) + jnp.where(has_down, 1, 0)

    flips = [jnp.bitwise_xor(matchings[m, group], group) for m in range(matches)]
    loads[0].wait()
    for at, b in enumerate(order):
        hits = [jnp.where(flips[m] == (1 << b), 1, 0) for m in range(matches)]
        which = jnp.minimum(sum(m * hits[m] for m in range(matches)), matches - 1)
        present = sum(hits)
        for i in range(parts):
            for j in range(parts):
                keep = (pair_mask[which, i, j] * present).astype(F32)
                block = pair_raw[which, pl.ds(i * BLK, BLK), pl.ds(j * BLK, BLK)]
                own[b, pl.ds(i * BLK, BLK), pl.ds(j * BLK, BLK)] = (block.astype(F32) * keep).astype(BF16)
        if at == 0:
            pl.semaphore_wait(barrier, neighbours)

        @pl.when(gives[b])
        def _():
            block_copy(b).start()

    def send_vectors(step, h):
        for b in order:
            @pl.when(gives[b])
            def _():
                given_copy(step, b, h).start()

        @pl.when(has_down)
        def _():
            down_copy(step, h).start()

    def send_lift(step, h):
        @pl.when(has_up)
        def _():
            lift[step, h] = mm(up_t[...], vec[step, h]).astype(BF16)
            rise_copy(step, h).start()

    def send_reply(step, b, h):
        reply[step, b, h] = mm(full_t[b], vec[step, h]).astype(BF16)
        reply_copy(step, b, h).start()

    for h in range(halves):
        loads[1 + h].wait()
        send_vectors(0, h)

    loads[1 + halves].wait()
    for i in range(parts):
        for j in range(parts):
            keep = shell_mask[i, j].astype(F32)
            block = shell_raw[pl.ds(i * BLK, BLK), pl.ds(j * BLK, BLK)].astype(F32) * keep
            up[pl.ds(i * BLK, BLK), pl.ds(j * BLK, BLK)] = block.astype(BF16)
            up_t[pl.ds(j * BLK, BLK), pl.ds(i * BLK, BLK)] = block.T.astype(BF16)
    for h in range(halves):
        send_lift(0, h)

    loads[2 + halves].wait()
    for i in range(parts):
        for j in range(parts):
            here, there = pl.ds(i * BLK, BLK), pl.ds(j * BLK, BLK)
            sym[here, there] = (local_raw[here, there].astype(F32) + turned(local_raw[there, here])).astype(BF16)

    def begin(step, h):
        v = vec[step, h]
        acc[step, h] = mm(sym[...], v) - spectrum_center * v.astype(F32)

    for h in range(halves):
        begin(0, h)

    for b in order:
        @pl.when(holds[b])
        def _():
            block_copy(b).wait_recv()
            for i in range(parts):
                for j in range(parts):
                    here, there = pl.ds(i * BLK, BLK), pl.ds(j * BLK, BLK)
                    k_t = theirs[b, here, there].astype(F32) + turned(own[b, there, here])
                    full_t[b, here, there] = k_t.astype(BF16)
                    full[b, there, here] = k_t.T.astype(BF16)
            for h in range(halves):
                send_reply(0, b, h)

    def gather(step, h):
        @pl.when(has_up)
        def _():
            down_copy(step, h).wait_recv()
            acc[step, h] += mm(up[...], from_up[step, h])

        @pl.when(has_down)
        def _():
            rise_copy(step, h).wait_recv()
            acc[step, h] += from_down[step, h].astype(F32)

        for b in reversed(order):
            @pl.when(holds[b])
            def _():
                given_copy(step, b, h).wait_recv()
                acc[step, h] += mm(full[b], arrived[step, b, h])

        for b in reversed(order):
            @pl.when(gives[b])
            def _():
                reply_copy(step, b, h).wait_recv()
                acc[step, h] += arrived[step, b, h].astype(F32)

    for h in range(halves):
        gather(0, h)
        vec[1, h] = (acc[0, h] * (1.0 / spectrum_halfwidth)).astype(BF16)
        send_vectors(1, h)
        for b in order:
            @pl.when(holds[b])
            def _():
                send_reply(1, b, h)
        send_lift(1, h)
        begin(1, h)

    stores = []
    for h in range(halves):
        gather(1, h)
        result[h] = (acc[1, h] * (2.0 / spectrum_halfwidth) - vec[0, h].astype(F32)).astype(BF16)
        store = pltpu.make_async_copy(result.at[h], out_hbm.at[:, columns(h)], out_sem.at[h])
        store.start()
        stores.append(store)

    for b in range(bits):
        @pl.when(gives[b])
        def _():
            block_copy(b).wait_send()
            for step in range(2):
                for h in range(halves):
                    given_copy(step, b, h).wait_send()

        @pl.when(holds[b])
        def _():
            for step in range(2):
                for h in range(halves):
                    reply_copy(step, b, h).wait_send()

    @pl.when(has_down)
    def _():
        for step in range(2):
            for h in range(halves):
                down_copy(step, h).wait_send()

    @pl.when(has_up)
    def _():
        for step in range(2):
            for h in range(halves):
                rise_copy(step, h).wait_send()

    for store in stores:
        store.wait()


def on_device(bits, shells, vectors, local_block, pair_blocks, pair_masks, shell_block, shell_mask, matchings):
    rows, width = vectors.shape[2:]
    matches = pair_blocks.shape[2]
    halves = width // LANES
    square = (rows, rows)
    tall = (halves, rows, LANES)
    out = pl.pallas_call(
        functools.partial(filter_kernel, bits, shells),
        out_shape=jax.ShapeDtypeStruct((rows, width), BF16),
        in_specs=[pl.BlockSpec(memory_space=pl.ANY)] * 4 + [pl.BlockSpec(memory_space=pltpu.SMEM)] * 3,
        out_specs=pl.BlockSpec(memory_space=pl.ANY),
        scratch_shapes=[
            pltpu.VMEM((2,) + tall, BF16),
            pltpu.VMEM(square, BF16),
            pltpu.VMEM((matches,) + square, BF16),
            pltpu.VMEM(square, BF16),
            pltpu.VMEM((bits,) + square, BF16),
            pltpu.VMEM((bits,) + square, BF16),
            pltpu.VMEM((bits,) + square, BF16),
            pltpu.VMEM((bits,) + square, BF16),
            pltpu.VMEM(square, BF16),
            pltpu.VMEM(square, BF16),
            pltpu.VMEM(square, BF16),
            pltpu.VMEM((2, bits) + tall, BF16),
            pltpu.VMEM((2, bits) + tall, BF16),
            pltpu.VMEM((2,) + tall, BF16),
            pltpu.VMEM((2,) + tall, BF16),
            pltpu.VMEM((2,) + tall, BF16),
            pltpu.VMEM((2,) + tall, F32),
            pltpu.VMEM(tall, BF16),
            pltpu.SemaphoreType.DMA((3 + halves,)),
            pltpu.SemaphoreType.DMA((halves,)),
            pltpu.SemaphoreType.DMA((bits,)),
            pltpu.SemaphoreType.DMA((bits,)),
            pltpu.SemaphoreType.DMA((2, bits, halves)),
            pltpu.SemaphoreType.DMA((2, bits, halves)),
            pltpu.SemaphoreType.DMA((2, halves)),
            pltpu.SemaphoreType.DMA((2, halves)),
            pltpu.SemaphoreType.DMA((2, halves)),
            pltpu.SemaphoreType.DMA((2, halves)),
        ],
        compiler_params=pltpu.CompilerParams(
            collective_id=0, has_side_effects=True, vmem_limit_bytes=40 * 1024 * 1024
        ),
    )(
        vectors[0, 0],
        local_block[0, 0],
        pair_blocks[0, 0],
        shell_block[0, 0],
        pair_masks[0, 0],
        shell_mask[0, 0],
        matchings,
    )
    return out[None, None]


def solution(mesh):
    sizes = dict(mesh.shape)
    bits = sizes["grp"].bit_length() - 1
    in_specs = (
        P("grp", "shell", None, None),
        P("grp", "shell", None, None),
        P("grp", "shell", None, None, None),
        P("grp", "shell", None, None, None),
        P("grp", "shell", None, None),
        P("grp", "shell", None, None),
        P(),
    )
    out_specs = P("grp", "shell", None, None)
    return jax.shard_map(
        functools.partial(on_device, bits, sizes["shell"]),
        mesh=mesh, in_specs=in_specs, out_specs=out_specs, check_vma=False,
    )
```

```python
import functools

import jax
import jax.numpy as jnp
from jax import lax
from jax.experimental import pallas as pl
from jax.experimental.pallas import tpu as pltpu
from jax.sharding import PartitionSpec as P

BLK = 128
LANES = 128

spectrum_center = 1.0
spectrum_halfwidth = 6.0

MESH = pl.DeviceIdType.MESH
F32 = jnp.float32
BF16 = jnp.bfloat16


def mm(a, b):
    return jnp.dot(a, b, preferred_element_type=F32)


def turned(x):
    return x.astype(F32).T


def filter_kernel(
    bits,
    shells,
    vec_hbm,
    local_hbm,
    pair_hbm,
    shell_hbm,
    pair_mask_hbm,
    shell_mask_hbm,
    matchings_hbm,
    out,
    pair_mask,
    shell_mask,
    matchings,
    vec,
    local_raw,
    pair_raw,
    shell_raw,
    own,
    theirs,
    full,
    full_t,
    sym,
    up,
    up_t,
    reply,
    arrived,
    lift,
    from_up,
    from_down,
    acc,
    load_sem,
    block_send,
    block_recv,
    edge_send,
    edge_recv,
    down_send,
    down_recv,
    rise_send,
    rise_recv,
):
    halves = vec.shape[1]
    rows = vec.shape[2]
    parts = rows // BLK
    matches = pair_raw.shape[0]
    group = lax.axis_index("grp")
    shell = lax.axis_index("shell")
    has_up = shell < shells - 1
    has_down = shell > 0
    order = list(reversed(range(bits)))

    def digit(b):
        return (group // (1 << b)) % 2

    partner = [group + (1 << b) - 2 * (1 << b) * digit(b) for b in range(bits)]
    role = [(digit(b) + (digit((b + 1) % bits) if bits > 1 else 0) + shell) % 2 for b in range(bits)]
    holds = [role[b] == 1 for b in range(bits)]
    gives = [role[b] == 0 for b in range(bits)]

    columns = lambda h: pl.ds(h * LANES, LANES)
    loads = [pltpu.make_async_copy(pair_hbm, pair_raw, load_sem.at[0])]
    for h in range(halves):
        loads.append(pltpu.make_async_copy(vec_hbm.at[:, columns(h)], vec.at[0, h], load_sem.at[1 + h]))
    loads.append(pltpu.make_async_copy(shell_hbm, shell_raw, load_sem.at[1 + halves]))
    loads.append(pltpu.make_async_copy(local_hbm, local_raw, load_sem.at[2 + halves]))
    tables = [
        pltpu.make_async_copy(matchings_hbm, matchings, load_sem.at[3 + halves]),
        pltpu.make_async_copy(pair_mask_hbm, pair_mask, load_sem.at[4 + halves]),
        pltpu.make_async_copy(shell_mask_hbm, shell_mask, load_sem.at[5 + halves]),
    ]
    for load in tables + loads:
        load.start()

    def block_copy(b):
        return pltpu.make_async_remote_copy(
            src_ref=own.at[b], dst_ref=theirs.at[b], send_sem=block_send.at[b], recv_sem=block_recv.at[b],
            device_id={"grp": partner[b]}, device_id_type=MESH)

    def edge_copy(source, step, b, h):
        return pltpu.make_async_remote_copy(
            src_ref=source, dst_ref=arrived.at[step, b, h], send_sem=edge_send.at[step, b, h],
            recv_sem=edge_recv.at[step, b, h], device_id={"grp": partner[b]}, device_id_type=MESH)

    def given_copy(step, b, h):
        return edge_copy(vec.at[step, h], step, b, h)

    def reply_copy(step, b, h):
        return edge_copy(reply.at[step, b, h], step, b, h)

    def down_copy(step, h):
        return pltpu.make_async_remote_copy(
            src_ref=vec.at[step, h], dst_ref=from_up.at[step, h], send_sem=down_send.at[step, h],
            recv_sem=down_recv.at[step, h], device_id={"shell": shell - 1}, device_id_type=MESH)

    def rise_copy(step, h):
        return pltpu.make_async_remote_copy(
            src_ref=lift.at[step, h], dst_ref=from_down.at[step, h], send_sem=rise_send.at[step, h],
            recv_sem=rise_recv.at[step, h], device_id={"shell": shell + 1}, device_id_type=MESH)

    barrier = pltpu.get_barrier_semaphore()
    for b in range(bits):
        pl.semaphore_signal(barrier, inc=1, device_id={"grp": partner[b]}, device_id_type=MESH)

    @pl.when(has_up)
    def _():
        pl.semaphore_signal(barrier, inc=1, device_id={"shell": shell + 1}, device_id_type=MESH)

    @pl.when(has_down)
    def _():
        pl.semaphore_signal(barrier, inc=1, device_id={"shell": shell - 1}, device_id_type=MESH)

    neighbours = bits + jnp.where(has_up, 1, 0) + jnp.where(has_down, 1, 0)

    for table in tables:
        table.wait()
    flips = [jnp.bitwise_xor(matchings[m, group], group) for m in range(matches)]
    loads[0].wait()
    for at, b in enumerate(order):
        hits = [jnp.where(flips[m] == (1 << b), 1, 0) for m in range(matches)]
        which = jnp.minimum(sum(m * hits[m] for m in range(matches)), matches - 1)
        present = sum(hits)
        for i in range(parts):
            for j in range(parts):
                keep = (pair_mask[which * parts + i, 0, j] * present).astype(F32)
                block = pair_raw[which, pl.ds(i * BLK, BLK), pl.ds(j * BLK, BLK)]
                own[b, pl.ds(i * BLK, BLK), pl.ds(j * BLK, BLK)] = (block.astype(F32) * keep).astype(BF16)
        if at == 0:
            pl.semaphore_wait(barrier, neighbours)

        @pl.when(gives[b])
        def _():
            block_copy(b).start()

    def send_vectors(step, h):
        for b in order:
            @pl.when(gives[b])
            def _():
                given_copy(step, b, h).start()

        @pl.when(has_down)
        def _():
            down_copy(step, h).start()

    def send_lift(step, h):
        @pl.when(has_up)
        def _():
            lift[step, h] = mm(up_t[...], vec[step, h]).astype(BF16)
            rise_copy(step, h).start()

    def send_reply(step, b, h):
        reply[step, b, h] = mm(full_t[b], vec[step, h]).astype(BF16)
        reply_copy(step, b, h).start()

    for h in range(halves):
        loads[1 + h].wait()
        send_vectors(0, h)

    loads[1 + halves].wait()
    for i in range(parts):
        for j in range(parts):
            keep = shell_mask[i, 0, j].astype(F32)
            block = shell_raw[pl.ds(i * BLK, BLK), pl.ds(j * BLK, BLK)].astype(F32) * keep
            up[pl.ds(i * BLK, BLK), pl.ds(j * BLK, BLK)] = block.astype(BF16)
            up_t[pl.ds(j * BLK, BLK), pl.ds(i * BLK, BLK)] = block.T.astype(BF16)
    for h in range(halves):
        send_lift(0, h)

    loads[2 + halves].wait()
    for i in range(parts):
        for j in range(parts):
            here, there = pl.ds(i * BLK, BLK), pl.ds(j * BLK, BLK)
            sym[here, there] = (local_raw[here, there].astype(F32) + turned(local_raw[there, here])).astype(BF16)

    def begin(step, h):
        v = vec[step, h]
        acc[step, h] = mm(sym[...], v) - spectrum_center * v.astype(F32)

    for h in range(halves):
        begin(0, h)

    def each_block(work):
        for i in range(parts):
            for j in range(parts):
                work(pl.ds(i * BLK, BLK), pl.ds(j * BLK, BLK))

    for b in range(bits):
        @pl.when(holds[b])
        def _():
            def turn(here, there):
                full_t[b, here, there] = turned(own[b, there, here]).astype(BF16)

            each_block(turn)

    for b in range(bits):
        @pl.when(holds[b])
        def _():
            def join(here, there):
                k_t = theirs[b, here, there].astype(F32) + full_t[b, here, there].astype(F32)
                full_t[b, here, there] = k_t.astype(BF16)

            block_copy(b).wait_recv()
            each_block(join)
            send_reply(0, b, 0)

    for h in range(1, halves):
        for b in order:
            @pl.when(holds[b])
            def _():
                send_reply(0, b, h)

    for b in range(bits):
        @pl.when(holds[b])
        def _():
            def turn_back(here, there):
                full[b, there, here] = turned(full_t[b, here, there]).astype(BF16)

            each_block(turn_back)

    def gather(step, h):
        @pl.when(has_up)
        def _():
            down_copy(step, h).wait_recv()
            acc[step, h] += mm(up[...], from_up[step, h])

        @pl.when(has_down)
        def _():
            rise_copy(step, h).wait_recv()
            acc[step, h] += from_down[step, h].astype(F32)

        for b in reversed(order):
            @pl.when(holds[b])
            def _():
                given_copy(step, b, h).wait_recv()
                acc[step, h] += mm(full[b], arrived[step, b, h])

        for b in reversed(order):
            @pl.when(gives[b])
            def _():
                reply_copy(step, b, h).wait_recv()
                acc[step, h] += arrived[step, b, h].astype(F32)

    for h in range(halves):
        gather(0, h)
        vec[1, h] = (acc[0, h] * (1.0 / spectrum_halfwidth)).astype(BF16)
        send_vectors(1, h)
        for b in order:
            @pl.when(holds[b])
            def _():
                send_reply(1, b, h)
        send_lift(1, h)
        begin(1, h)

    for h in range(halves):
        gather(1, h)
        y2 = acc[1, h] * (2.0 / spectrum_halfwidth) - vec[0, h].astype(F32)
        out[:, columns(h)] = y2.astype(BF16)

    for b in range(bits):
        @pl.when(gives[b])
        def _():
            block_copy(b).wait_send()
            for step in range(2):
                for h in range(halves):
                    given_copy(step, b, h).wait_send()

        @pl.when(holds[b])
        def _():
            for step in range(2):
                for h in range(halves):
                    reply_copy(step, b, h).wait_send()

    @pl.when(has_down)
    def _():
        for step in range(2):
            for h in range(halves):
                down_copy(step, h).wait_send()

    @pl.when(has_up)
    def _():
        for step in range(2):
            for h in range(halves):
                rise_copy(step, h).wait_send()


def on_device(bits, shells, vectors, local_block, pair_blocks, pair_masks, shell_block, shell_mask, matchings):
    rows, width = vectors.shape[2:]
    matches = pair_blocks.shape[2]
    halves = width // LANES
    parts = pair_masks.shape[-1]
    pair_masks = pair_masks.reshape(matches * parts, 1, parts)
    shell_mask = shell_mask.reshape(parts, 1, parts)
    square = (rows, rows)
    tall = (halves, rows, LANES)
    out = pl.pallas_call(
        functools.partial(filter_kernel, bits, shells),
        out_shape=jax.ShapeDtypeStruct((rows, width), BF16),
        in_specs=[pl.BlockSpec(memory_space=pltpu.HBM)] * 7,
        out_specs=pl.BlockSpec(memory_space=pltpu.VMEM),
        scratch_shapes=[
            pltpu.SMEM(pair_masks.shape, jnp.int32),
            pltpu.SMEM(shell_mask.shape, jnp.int32),
            pltpu.SMEM(matchings.shape, jnp.int32),
            pltpu.VMEM((2,) + tall, BF16),
            pltpu.VMEM(square, BF16),
            pltpu.VMEM((matches,) + square, BF16),
            pltpu.VMEM(square, BF16),
            pltpu.VMEM((bits,) + square, BF16),
            pltpu.VMEM((bits,) + square, BF16),
            pltpu.VMEM((bits,) + square, BF16),
            pltpu.VMEM((bits,) + square, BF16),
            pltpu.VMEM(square, BF16),
            pltpu.VMEM(square, BF16),
            pltpu.VMEM(square, BF16),
            pltpu.VMEM((2, bits) + tall, BF16),
            pltpu.VMEM((2, bits) + tall, BF16),
            pltpu.VMEM((2,) + tall, BF16),
            pltpu.VMEM((2,) + tall, BF16),
            pltpu.VMEM((2,) + tall, BF16),
            pltpu.VMEM((2,) + tall, F32),
            pltpu.SemaphoreType.DMA((6 + halves,)),
            pltpu.SemaphoreType.DMA((bits,)),
            pltpu.SemaphoreType.DMA((bits,)),
            pltpu.SemaphoreType.DMA((2, bits, halves)),
            pltpu.SemaphoreType.DMA((2, bits, halves)),
            pltpu.SemaphoreType.DMA((2, halves)),
            pltpu.SemaphoreType.DMA((2, halves)),
            pltpu.SemaphoreType.DMA((2, halves)),
            pltpu.SemaphoreType.DMA((2, halves)),
        ],
        compiler_params=pltpu.CompilerParams(
            collective_id=0, has_side_effects=True, vmem_limit_bytes=int(63.5 * 1024 * 1024)
        ),
    )(
        vectors[0, 0],
        local_block[0, 0],
        pair_blocks[0, 0],
        shell_block[0, 0],
        pair_masks,
        shell_mask,
        matchings,
    )
    return out[None, None]


def solution(mesh):
    sizes = dict(mesh.shape)
    bits = sizes["grp"].bit_length() - 1
    in_specs = (
        P("grp", "shell", None, None),
        P("grp", "shell", None, None),
        P("grp", "shell", None, None, None),
        P("grp", "shell", None, None, None),
        P("grp", "shell", None, None),
        P("grp", "shell", None, None),
        P(),
    )
    out_specs = P("grp", "shell", None, None)
    return jax.shard_map(
        functools.partial(on_device, bits, sizes["shell"]),
        mesh=mesh, in_specs=in_specs, out_specs=out_specs, check_vma=False,
    )
```

```python
import functools

import jax
import jax.numpy as jnp
from jax import lax
from jax.experimental import pallas as pl
from jax.experimental.pallas import tpu as pltpu
from jax.sharding import PartitionSpec as P

BLK = 128
LANES = 128

spectrum_center = 1.0
spectrum_halfwidth = 6.0

MESH = pl.DeviceIdType.MESH
F32 = jnp.float32
BF16 = jnp.bfloat16


def mm(a, b):
    return jnp.dot(a, b, preferred_element_type=F32)


def turned(x):
    return x.astype(F32).T


def filter_kernel(
    bits,
    shells,
    vec_hbm,
    local_hbm,
    pair_hbm,
    shell_hbm,
    pair_mask_hbm,
    shell_mask_hbm,
    matchings_hbm,
    out,
    pair_mask,
    shell_mask,
    matchings,
    vec,
    local_raw,
    pair_raw,
    shell_raw,
    own,
    theirs,
    full,
    full_t,
    sym,
    up,
    up_t,
    reply,
    arrived,
    lift,
    from_up,
    from_down,
    acc,
    load_sem,
    block_send,
    block_recv,
    edge_send,
    edge_recv,
    down_send,
    down_recv,
    rise_send,
    rise_recv,
):
    halves = vec.shape[1]
    rows = vec.shape[2]
    parts = rows // BLK
    matches = pair_raw.shape[0]
    group = lax.axis_index("grp")
    shell = lax.axis_index("shell")
    has_up = shell < shells - 1
    has_down = shell > 0
    order = list(reversed(range(bits)))

    def digit(b):
        return (group // (1 << b)) % 2

    partner = [group + (1 << b) - 2 * (1 << b) * digit(b) for b in range(bits)]
    role = [(digit(b) + (digit((b + 1) % bits) if bits > 1 else 0) + shell) % 2 for b in range(bits)]
    holds = [role[b] == 1 for b in range(bits)]
    gives = [role[b] == 0 for b in range(bits)]

    columns = lambda h: pl.ds(h * LANES, LANES)
    loads = [pltpu.make_async_copy(pair_hbm, pair_raw, load_sem.at[0])]
    for h in range(halves):
        loads.append(pltpu.make_async_copy(vec_hbm.at[:, columns(h)], vec.at[0, h], load_sem.at[1 + h]))
    loads.append(pltpu.make_async_copy(shell_hbm, shell_raw, load_sem.at[1 + halves]))
    loads.append(pltpu.make_async_copy(local_hbm, local_raw, load_sem.at[2 + halves]))
    tables = [
        pltpu.make_async_copy(matchings_hbm, matchings, load_sem.at[3 + halves]),
        pltpu.make_async_copy(pair_mask_hbm, pair_mask, load_sem.at[4 + halves]),
        pltpu.make_async_copy(shell_mask_hbm, shell_mask, load_sem.at[5 + halves]),
    ]
    for load in tables + loads:
        load.start()

    def block_copy(b):
        return pltpu.make_async_remote_copy(
            src_ref=own.at[b], dst_ref=theirs.at[b], send_sem=block_send.at[b], recv_sem=block_recv.at[b],
            device_id={"grp": partner[b]}, device_id_type=MESH)

    def edge_copy(source, step, b, h):
        return pltpu.make_async_remote_copy(
            src_ref=source, dst_ref=arrived.at[step, b, h], send_sem=edge_send.at[step, b, h],
            recv_sem=edge_recv.at[step, b, h], device_id={"grp": partner[b]}, device_id_type=MESH)

    def given_copy(step, b, h):
        return edge_copy(vec.at[step, h], step, b, h)

    def reply_copy(step, b, h):
        return edge_copy(reply.at[step, b, h], step, b, h)

    def down_copy(step, h):
        return pltpu.make_async_remote_copy(
            src_ref=vec.at[step, h], dst_ref=from_up.at[step, h], send_sem=down_send.at[step, h],
            recv_sem=down_recv.at[step, h], device_id={"shell": shell - 1}, device_id_type=MESH)

    def rise_copy(step, h):
        return pltpu.make_async_remote_copy(
            src_ref=lift.at[step, h], dst_ref=from_down.at[step, h], send_sem=rise_send.at[step, h],
            recv_sem=rise_recv.at[step, h], device_id={"shell": shell + 1}, device_id_type=MESH)

    barrier = pltpu.get_barrier_semaphore()
    for b in range(bits):
        pl.semaphore_signal(barrier, inc=1, device_id={"grp": partner[b]}, device_id_type=MESH)

    @pl.when(has_up)
    def _():
        pl.semaphore_signal(barrier, inc=1, device_id={"shell": shell + 1}, device_id_type=MESH)

    @pl.when(has_down)
    def _():
        pl.semaphore_signal(barrier, inc=1, device_id={"shell": shell - 1}, device_id_type=MESH)

    neighbours = bits + jnp.where(has_up, 1, 0) + jnp.where(has_down, 1, 0)

    for table in tables:
        table.wait()
    flips = [jnp.bitwise_xor(matchings[m, group], group) for m in range(matches)]
    loads[0].wait()
    for at, b in enumerate(order):
        hits = [jnp.where(flips[m] == (1 << b), 1, 0) for m in range(matches)]
        which = jnp.minimum(sum(m * hits[m] for m in range(matches)), matches - 1)
        present = sum(hits)
        for i in range(parts):
            for j in range(parts):
                keep = (pair_mask[which * parts + i, 0, j] * present).astype(F32)
                block = pair_raw[which, pl.ds(i * BLK, BLK), pl.ds(j * BLK, BLK)]
                own[b, pl.ds(i * BLK, BLK), pl.ds(j * BLK, BLK)] = (block.astype(F32) * keep).astype(BF16)
        if at == 0:
            pl.semaphore_wait(barrier, neighbours)

        @pl.when(gives[b])
        def _():
            block_copy(b).start()

    def send_vectors(step, h):
        for b in order:
            @pl.when(gives[b])
            def _():
                given_copy(step, b, h).start()

        @pl.when(has_down)
        def _():
            down_copy(step, h).start()

    def send_lift(step, h):
        @pl.when(has_up)
        def _():
            lift[step, h] = mm(up_t[...], vec[step, h]).astype(BF16)
            rise_copy(step, h).start()

    def send_reply(step, b, h):
        reply[step, b, h] = mm(full_t[b], vec[step, h]).astype(BF16)
        reply_copy(step, b, h).start()

    for h in range(halves):
        loads[1 + h].wait()
        send_vectors(0, h)

    loads[1 + halves].wait()
    for i in range(parts):
        for j in range(parts):
            keep = shell_mask[i, 0, j].astype(F32)
            block = shell_raw[pl.ds(i * BLK, BLK), pl.ds(j * BLK, BLK)].astype(F32) * keep
            up[pl.ds(i * BLK, BLK), pl.ds(j * BLK, BLK)] = block.astype(BF16)
            up_t[pl.ds(j * BLK, BLK), pl.ds(i * BLK, BLK)] = block.T.astype(BF16)
    for h in range(halves):
        send_lift(0, h)

    loads[2 + halves].wait()
    for i in range(parts):
        for j in range(parts):
            here, there = pl.ds(i * BLK, BLK), pl.ds(j * BLK, BLK)
            sym[here, there] = (local_raw[here, there].astype(F32) + turned(local_raw[there, here])).astype(BF16)

    def begin(step, h):
        v = vec[step, h]
        acc[step, h] = mm(sym[...], v) - spectrum_center * v.astype(F32)

    for h in range(halves):
        begin(0, h)

    def each_block(work):
        for i in range(parts):
            for j in range(parts):
                work(pl.ds(i * BLK, BLK), pl.ds(j * BLK, BLK))

    for b in range(bits):
        @pl.when(holds[b])
        def _():
            def turn(here, there):
                full_t[b, here, there] = turned(own[b, there, here]).astype(BF16)

            each_block(turn)

    for b in range(bits):
        @pl.when(holds[b])
        def _():
            def join(here, there):
                k_t = theirs[b, here, there].astype(F32) + full_t[b, here, there].astype(F32)
                full_t[b, here, there] = k_t.astype(BF16)

            block_copy(b).wait_recv()
            each_block(join)
            send_reply(0, b, 0)

    for h in range(1, halves):
        for b in order:
            @pl.when(holds[b])
            def _():
                send_reply(0, b, h)

    for b in range(bits):
        @pl.when(holds[b])
        def _():
            def turn_back(here, there):
                full[b, there, here] = turned(full_t[b, here, there]).astype(BF16)

            each_block(turn_back)

    def gather(step, h):
        @pl.when(has_up)
        def _():
            down_copy(step, h).wait_recv()
            acc[step, h] += mm(up[...], from_up[step, h])

        @pl.when(has_down)
        def _():
            rise_copy(step, h).wait_recv()
            acc[step, h] += from_down[step, h].astype(F32)

        for b in reversed(order):
            @pl.when(holds[b])
            def _():
                given_copy(step, b, h).wait_recv()
                acc[step, h] += mm(full[b], arrived[step, b, h])

        for b in reversed(order):
            @pl.when(gives[b])
            def _():
                reply_copy(step, b, h).wait_recv()
                acc[step, h] += arrived[step, b, h].astype(F32)

    for h in range(halves):
        gather(0, h)
        vec[1, h] = (acc[0, h] * (1.0 / spectrum_halfwidth)).astype(BF16)
        send_vectors(1, h)
        for b in order:
            @pl.when(holds[b])
            def _():
                send_reply(1, b, h)
        send_lift(1, h)
        begin(1, h)

    for h in range(halves):
        gather(1, h)
        y2 = acc[1, h] * (2.0 / spectrum_halfwidth) - vec[0, h].astype(F32)
        out[:, columns(h)] = y2.astype(BF16)

    for b in range(bits):
        @pl.when(gives[b])
        def _():
            block_copy(b).wait_send()
            for step in range(2):
                for h in range(halves):
                    given_copy(step, b, h).wait_send()

        @pl.when(holds[b])
        def _():
            for step in range(2):
                for h in range(halves):
                    reply_copy(step, b, h).wait_send()

    @pl.when(has_down)
    def _():
        for step in range(2):
            for h in range(halves):
                down_copy(step, h).wait_send()

    @pl.when(has_up)
    def _():
        for step in range(2):
            for h in range(halves):
                rise_copy(step, h).wait_send()


def on_device(bits, shells, vectors, local_block, pair_blocks, pair_masks, shell_block, shell_mask, matchings):
    rows, width = vectors.shape[2:]
    matches = pair_blocks.shape[2]
    halves = width // LANES
    parts = pair_masks.shape[-1]
    pair_masks = pair_masks.reshape(matches * parts, 1, parts)
    shell_mask = shell_mask.reshape(parts, 1, parts)
    square = (rows, rows)
    tall = (halves, rows, LANES)
    out = pl.pallas_call(
        functools.partial(filter_kernel, bits, shells),
        out_shape=jax.ShapeDtypeStruct((rows, width), BF16),
        in_specs=[pl.BlockSpec(memory_space=pltpu.HBM)] * 7,
        out_specs=pl.BlockSpec(memory_space=pltpu.VMEM),
        scratch_shapes=[
            pltpu.SMEM(pair_masks.shape, jnp.int32),
            pltpu.SMEM(shell_mask.shape, jnp.int32),
            pltpu.SMEM(matchings.shape, jnp.int32),
            pltpu.VMEM((2,) + tall, BF16),
            pltpu.VMEM(square, BF16),
            pltpu.VMEM((matches,) + square, BF16),
            pltpu.VMEM(square, BF16),
            pltpu.VMEM((bits,) + square, BF16),
            pltpu.VMEM((bits,) + square, BF16),
            pltpu.VMEM((bits,) + square, BF16),
            pltpu.VMEM((bits,) + square, BF16),
            pltpu.VMEM(square, BF16),
            pltpu.VMEM(square, BF16),
            pltpu.VMEM(square, BF16),
            pltpu.VMEM((2, bits) + tall, BF16),
            pltpu.VMEM((2, bits) + tall, BF16),
            pltpu.VMEM((2,) + tall, BF16),
            pltpu.VMEM((2,) + tall, BF16),
            pltpu.VMEM((2,) + tall, BF16),
            pltpu.VMEM((2,) + tall, F32),
            pltpu.SemaphoreType.DMA((6 + halves,)),
            pltpu.SemaphoreType.DMA((bits,)),
            pltpu.SemaphoreType.DMA((bits,)),
            pltpu.SemaphoreType.DMA((2, bits, halves)),
            pltpu.SemaphoreType.DMA((2, bits, halves)),
            pltpu.SemaphoreType.DMA((2, halves)),
            pltpu.SemaphoreType.DMA((2, halves)),
            pltpu.SemaphoreType.DMA((2, halves)),
            pltpu.SemaphoreType.DMA((2, halves)),
        ],
        compiler_params=pltpu.CompilerParams(
            collective_id=0, has_side_effects=True, vmem_limit_bytes=40 * 1024 * 1024
        ),
    )(*[
        pltpu.with_memory_space_constraint(x, pltpu.HBM)
        for x in (
            vectors[0, 0],
            local_block[0, 0],
            pair_blocks[0, 0],
            shell_block[0, 0],
            pair_masks,
            shell_mask,
            matchings,
        )
    ])
    return out[None, None]


def solution(mesh):
    sizes = dict(mesh.shape)
    bits = sizes["grp"].bit_length() - 1
    in_specs = (
        P("grp", "shell", None, None),
        P("grp", "shell", None, None),
        P("grp", "shell", None, None, None),
        P("grp", "shell", None, None, None),
        P("grp", "shell", None, None),
        P("grp", "shell", None, None),
        P(),
    )
    out_specs = P("grp", "shell", None, None)
    return jax.shard_map(
        functools.partial(on_device, bits, sizes["shell"]),
        mesh=mesh, in_specs=in_specs, out_specs=out_specs, check_vma=False,
    )
```

```python
import functools

import jax
import jax.numpy as jnp
from jax import lax
from jax.experimental import pallas as pl
from jax.experimental.pallas import tpu as pltpu
from jax.sharding import PartitionSpec as P

BLK = 128
LANES = 128

spectrum_center = 1.0
spectrum_halfwidth = 6.0

MESH = pl.DeviceIdType.MESH
F32 = jnp.float32
BF16 = jnp.bfloat16


def mm(a, b):
    return jnp.dot(a, b, preferred_element_type=F32)


def filter_kernel(
    bits,
    shells,
    vec_hbm,
    local_hbm,
    pair_hbm,
    shell_hbm,
    pair_mask_hbm,
    shell_mask_hbm,
    matchings_hbm,
    out,
    pair_mask,
    shell_mask,
    matchings,
    vec,
    local_raw,
    pair_raw,
    shell_raw,
    own,
    theirs,
    full,
    full_t,
    sym,
    up,
    up_t,
    reply,
    arrived,
    lift,
    from_up,
    from_down,
    acc,
    load_sem,
    block_send,
    block_recv,
    edge_send,
    edge_recv,
    down_send,
    down_recv,
    rise_send,
    rise_recv,
):
    halves = vec.shape[1]
    rows = vec.shape[2]
    parts = rows // BLK
    matches = pair_raw.shape[0]
    group = lax.axis_index("grp")
    shell = lax.axis_index("shell")
    has_up = shell < shells - 1
    has_down = shell > 0
    order = list(reversed(range(bits)))

    def digit(b):
        return (group // (1 << b)) % 2

    partner = [group + (1 << b) - 2 * (1 << b) * digit(b) for b in range(bits)]
    role = [(digit(b) + (digit((b + 1) % bits) if bits > 1 else 0) + shell) % 2 for b in range(bits)]
    holds = [role[b] == 1 for b in range(bits)]
    gives = [role[b] == 0 for b in range(bits)]

    columns = lambda h: pl.ds(h * LANES, LANES)
    loads = [pltpu.make_async_copy(pair_hbm, pair_raw, load_sem.at[0])]
    for h in range(halves):
        loads.append(pltpu.make_async_copy(vec_hbm.at[:, columns(h)], vec.at[0, h], load_sem.at[1 + h]))
    loads.append(pltpu.make_async_copy(shell_hbm, shell_raw, load_sem.at[1 + halves]))
    loads.append(pltpu.make_async_copy(local_hbm, local_raw, load_sem.at[2 + halves]))
    tables = [
        pltpu.make_async_copy(matchings_hbm, matchings, load_sem.at[3 + halves]),
        pltpu.make_async_copy(pair_mask_hbm, pair_mask, load_sem.at[4 + halves]),
        pltpu.make_async_copy(shell_mask_hbm, shell_mask, load_sem.at[5 + halves]),
    ]
    for load in tables + loads:
        load.start()

    def block_copy(b):
        return pltpu.make_async_remote_copy(
            src_ref=own.at[b], dst_ref=theirs.at[b], send_sem=block_send.at[b], recv_sem=block_recv.at[b],
            device_id={"grp": partner[b]}, device_id_type=MESH)

    def edge_copy(source, step, b, h):
        return pltpu.make_async_remote_copy(
            src_ref=source, dst_ref=arrived.at[step, b, h], send_sem=edge_send.at[step, b, h],
            recv_sem=edge_recv.at[step, b, h], device_id={"grp": partner[b]}, device_id_type=MESH)

    def given_copy(step, b, h):
        return edge_copy(vec.at[step, h], step, b, h)

    def reply_copy(step, b, h):
        return edge_copy(reply.at[step, b, h], step, b, h)

    def down_copy(step, h):
        return pltpu.make_async_remote_copy(
            src_ref=vec.at[step, h], dst_ref=from_up.at[step, h], send_sem=down_send.at[step, h],
            recv_sem=down_recv.at[step, h], device_id={"shell": shell - 1}, device_id_type=MESH)

    def rise_copy(step, h):
        return pltpu.make_async_remote_copy(
            src_ref=lift.at[step, h], dst_ref=from_down.at[step, h], send_sem=rise_send.at[step, h],
            recv_sem=rise_recv.at[step, h], device_id={"shell": shell + 1}, device_id_type=MESH)

    barrier = pltpu.get_barrier_semaphore()
    for b in range(bits):
        pl.semaphore_signal(barrier, inc=1, device_id={"grp": partner[b]}, device_id_type=MESH)

    @pl.when(has_up)
    def _():
        pl.semaphore_signal(barrier, inc=1, device_id={"shell": shell + 1}, device_id_type=MESH)

    @pl.when(has_down)
    def _():
        pl.semaphore_signal(barrier, inc=1, device_id={"shell": shell - 1}, device_id_type=MESH)

    neighbours = bits + jnp.where(has_up, 1, 0) + jnp.where(has_down, 1, 0)

    def send_down(step, h):
        @pl.when(has_down)
        def _():
            down_copy(step, h).start()

    def send_vectors(step, h):
        for b in order:
            @pl.when(gives[b])
            def _():
                given_copy(step, b, h).start()

        send_down(step, h)

    def send_lift(step, h):
        @pl.when(has_up)
        def _():
            lift[step, h] = mm(up_t[...], vec[step, h]).astype(BF16)
            rise_copy(step, h).start()

    def send_reply(step, b, h):
        reply[step, b, h] = mm(full_t[b], vec[step, h]).astype(BF16)
        reply_copy(step, b, h).start()

    loads[1].wait()
    pl.semaphore_wait(barrier, neighbours)
    send_vectors(0, 0)

    for table in tables:
        table.wait()
    flips = [jnp.bitwise_xor(matchings[m, group], group) for m in range(matches)]
    loads[0].wait()
    for b in order:
        hits = [jnp.where(flips[m] == (1 << b), 1, 0) for m in range(matches)]
        which = jnp.minimum(sum(m * hits[m] for m in range(matches)), matches - 1)
        present = sum(hits)
        for i in range(parts):
            for j in range(parts):
                keep = (pair_mask[which * parts + i, 0, j] * present).astype(F32)
                keep = jnp.broadcast_to(keep, (BLK, BLK)).astype(BF16)
                block = pair_raw[which, pl.ds(i * BLK, BLK), pl.ds(j * BLK, BLK)]
                own[b, pl.ds(i * BLK, BLK), pl.ds(j * BLK, BLK)] = block * keep

        @pl.when(gives[b])
        def _():
            block_copy(b).start()

    for h in range(1, halves):
        loads[1 + h].wait()
        send_down(0, h)

    loads[1 + halves].wait()
    for i in range(parts):
        for j in range(parts):
            keep = jnp.broadcast_to(shell_mask[i, 0, j].astype(F32), (BLK, BLK)).astype(BF16)
            block = shell_raw[pl.ds(i * BLK, BLK), pl.ds(j * BLK, BLK)] * keep
            up[pl.ds(i * BLK, BLK), pl.ds(j * BLK, BLK)] = block
            up_t[pl.ds(j * BLK, BLK), pl.ds(i * BLK, BLK)] = block.T
    for h in range(halves):
        send_lift(0, h)

    loads[2 + halves].wait()
    for i in range(parts):
        for j in range(parts):
            here, there = pl.ds(i * BLK, BLK), pl.ds(j * BLK, BLK)
            sym[here, there] = (local_raw[here, there].astype(F32) + local_raw[there, here].T.astype(F32)).astype(BF16)

    def begin(step, h):
        v = vec[step, h]
        acc[step, h] = mm(sym[...], v) - spectrum_center * v.astype(F32)

    for h in range(halves):
        begin(0, h)

    def each_block(work):
        for i in range(parts):
            for j in range(parts):
                work(pl.ds(i * BLK, BLK), pl.ds(j * BLK, BLK))

    for b in range(bits):
        @pl.when(holds[b])
        def _():
            def turn(here, there):
                full_t[b, here, there] = own[b, there, here].T

            each_block(turn)

    for b in range(bits):
        @pl.when(holds[b])
        def _():
            def join(here, there):
                k_t = theirs[b, here, there].astype(F32) + full_t[b, here, there].astype(F32)
                full_t[b, here, there] = k_t.astype(BF16)

            block_copy(b).wait_recv()
            each_block(join)
            send_reply(0, b, 0)

        if b == 0:
            for c in order:
                @pl.when(gives[c])
                def _():
                    block_copy(c).wait_send()
                    for h in range(1, halves):
                        given_copy(0, c, h).start()

    for h in range(1, halves):
        for b in order:
            @pl.when(holds[b])
            def _():
                send_reply(0, b, h)

    for b in range(bits):
        @pl.when(holds[b])
        def _():
            def turn_back(here, there):
                full[b, there, here] = full_t[b, here, there].T

            each_block(turn_back)

    def gather(step, h):
        @pl.when(has_up)
        def _():
            down_copy(step, h).wait_recv()
            acc[step, h] += mm(up[...], from_up[step, h])

        @pl.when(has_down)
        def _():
            rise_copy(step, h).wait_recv()
            acc[step, h] += from_down[step, h].astype(F32)

        for b in reversed(order):
            @pl.when(holds[b])
            def _():
                given_copy(step, b, h).wait_recv()
                acc[step, h] += mm(full[b], arrived[step, b, h])

        for b in reversed(order):
            @pl.when(gives[b])
            def _():
                reply_copy(step, b, h).wait_recv()
                acc[step, h] += arrived[step, b, h].astype(F32)

    for h in range(halves):
        gather(0, h)
        vec[1, h] = (acc[0, h] * (1.0 / spectrum_halfwidth)).astype(BF16)
        send_vectors(1, h)
        for b in order:
            @pl.when(holds[b])
            def _():
                send_reply(1, b, h)
        send_lift(1, h)
        begin(1, h)

    for h in range(halves):
        gather(1, h)
        y2 = acc[1, h] * (2.0 / spectrum_halfwidth) - vec[0, h].astype(F32)
        out[:, columns(h)] = y2.astype(BF16)

    for b in range(bits):
        @pl.when(gives[b])
        def _():
            for step in range(2):
                for h in range(halves):
                    given_copy(step, b, h).wait_send()

        @pl.when(holds[b])
        def _():
            for step in range(2):
                for h in range(halves):
                    reply_copy(step, b, h).wait_send()

    @pl.when(has_down)
    def _():
        for step in range(2):
            for h in range(halves):
                down_copy(step, h).wait_send()

    @pl.when(has_up)
    def _():
        for step in range(2):
            for h in range(halves):
                rise_copy(step, h).wait_send()


def on_device(bits, shells, vectors, local_block, pair_blocks, pair_masks, shell_block, shell_mask, matchings):
    rows, width = vectors.shape[2:]
    matches = pair_blocks.shape[2]
    halves = width // LANES
    parts = pair_masks.shape[-1]
    pair_masks = pair_masks.reshape(matches * parts, 1, parts)
    shell_mask = shell_mask.reshape(parts, 1, parts)
    square = (rows, rows)
    tall = (halves, rows, LANES)
    out = pl.pallas_call(
        functools.partial(filter_kernel, bits, shells),
        out_shape=jax.ShapeDtypeStruct((rows, width), BF16),
        in_specs=[pl.BlockSpec(memory_space=pltpu.HBM)] * 7,
        out_specs=pl.BlockSpec(memory_space=pltpu.VMEM),
        scratch_shapes=[
            pltpu.SMEM(pair_masks.shape, jnp.int32),
            pltpu.SMEM(shell_mask.shape, jnp.int32),
            pltpu.SMEM(matchings.shape, jnp.int32),
            pltpu.VMEM((2,) + tall, BF16),
            pltpu.VMEM(square, BF16),
            pltpu.VMEM((matches,) + square, BF16),
            pltpu.VMEM(square, BF16),
            pltpu.VMEM((bits,) + square, BF16),
            pltpu.VMEM((bits,) + square, BF16),
            pltpu.VMEM((bits,) + square, BF16),
            pltpu.VMEM((bits,) + square, BF16),
            pltpu.VMEM(square, BF16),
            pltpu.VMEM(square, BF16),
            pltpu.VMEM(square, BF16),
            pltpu.VMEM((2, bits) + tall, BF16),
            pltpu.VMEM((2, bits) + tall, BF16),
            pltpu.VMEM((2,) + tall, BF16),
            pltpu.VMEM((2,) + tall, BF16),
            pltpu.VMEM((2,) + tall, BF16),
            pltpu.VMEM((2,) + tall, F32),
            pltpu.SemaphoreType.DMA((6 + halves,)),
            pltpu.SemaphoreType.DMA((bits,)),
            pltpu.SemaphoreType.DMA((bits,)),
            pltpu.SemaphoreType.DMA((2, bits, halves)),
            pltpu.SemaphoreType.DMA((2, bits, halves)),
            pltpu.SemaphoreType.DMA((2, halves)),
            pltpu.SemaphoreType.DMA((2, halves)),
            pltpu.SemaphoreType.DMA((2, halves)),
            pltpu.SemaphoreType.DMA((2, halves)),
        ],
        compiler_params=pltpu.CompilerParams(
            collective_id=0, has_side_effects=True, vmem_limit_bytes=40 * 1024 * 1024
        ),
    )(*[
        pltpu.with_memory_space_constraint(x, pltpu.HBM)
        for x in (
            vectors[0, 0],
            local_block[0, 0],
            pair_blocks[0, 0],
            shell_block[0, 0],
            pair_masks,
            shell_mask,
            matchings,
        )
    ])
    return out[None, None]


def solution(mesh):
    sizes = dict(mesh.shape)
    bits = sizes["grp"].bit_length() - 1
    in_specs = (
        P("grp", "shell", None, None),
        P("grp", "shell", None, None),
        P("grp", "shell", None, None, None),
        P("grp", "shell", None, None, None),
        P("grp", "shell", None, None),
        P("grp", "shell", None, None),
        P(),
    )
    out_specs = P("grp", "shell", None, None)
    return jax.shard_map(
        functools.partial(on_device, bits, sizes["shell"]),
        mesh=mesh, in_specs=in_specs, out_specs=out_specs, check_vma=False,
    )
```

```python
import functools

import jax
import jax.numpy as jnp
from jax import lax
from jax.experimental import pallas as pl
from jax.experimental.pallas import tpu as pltpu
from jax.sharding import PartitionSpec as P

BLK = 128
LANES = 128

spectrum_center = 1.0
spectrum_halfwidth = 6.0

MESH = pl.DeviceIdType.MESH
F32 = jnp.float32
BF16 = jnp.bfloat16


def mm(a, b):
    return jnp.dot(a, b, preferred_element_type=F32)


def filter_kernel(
    bits,
    shells,
    vec_hbm,
    local_hbm,
    pair_hbm,
    shell_hbm,
    pair_mask_hbm,
    shell_mask_hbm,
    matchings_hbm,
    out,
    pair_mask,
    shell_mask,
    matchings,
    vec,
    local_raw,
    pair_raw,
    shell_raw,
    own,
    theirs,
    full,
    full_t,
    sym,
    up,
    up_t,
    reply,
    arrived,
    lift,
    from_up,
    from_down,
    acc,
    load_sem,
    block_send,
    block_recv,
    edge_send,
    edge_recv,
    down_send,
    down_recv,
    rise_send,
    rise_recv,
):
    halves = vec.shape[1]
    rows = vec.shape[2]
    parts = rows // BLK
    matches = pair_raw.shape[0]
    group = lax.axis_index("grp")
    shell = lax.axis_index("shell")
    has_up = shell < shells - 1
    has_down = shell > 0
    order = list(reversed(range(bits)))

    def digit(b):
        return (group // (1 << b)) % 2

    partner = [group + (1 << b) - 2 * (1 << b) * digit(b) for b in range(bits)]
    role = [(digit(b) + (digit((b + 1) % bits) if bits > 1 else 0) + shell) % 2 for b in range(bits)]
    holds = [role[b] == 1 for b in range(bits)]
    gives = [role[b] == 0 for b in range(bits)]

    columns = lambda h: pl.ds(h * LANES, LANES)
    loads = [pltpu.make_async_copy(pair_hbm, pair_raw, load_sem.at[0])]
    for h in range(halves):
        loads.append(pltpu.make_async_copy(vec_hbm.at[:, columns(h)], vec.at[0, h], load_sem.at[1 + h]))
    loads.append(pltpu.make_async_copy(shell_hbm, shell_raw, load_sem.at[1 + halves]))
    loads.append(pltpu.make_async_copy(local_hbm, local_raw, load_sem.at[2 + halves]))
    tables = [
        pltpu.make_async_copy(matchings_hbm, matchings, load_sem.at[3 + halves]),
        pltpu.make_async_copy(pair_mask_hbm, pair_mask, load_sem.at[4 + halves]),
        pltpu.make_async_copy(shell_mask_hbm, shell_mask, load_sem.at[5 + halves]),
    ]
    for load in tables + loads:
        load.start()

    def block_copy(b):
        return pltpu.make_async_remote_copy(
            src_ref=own.at[b], dst_ref=theirs.at[b], send_sem=block_send.at[b], recv_sem=block_recv.at[b],
            device_id={"grp": partner[b]}, device_id_type=MESH)

    def edge_copy(source, step, b, h):
        return pltpu.make_async_remote_copy(
            src_ref=source, dst_ref=arrived.at[step, b, h], send_sem=edge_send.at[step, b, h],
            recv_sem=edge_recv.at[step, b, h], device_id={"grp": partner[b]}, device_id_type=MESH)

    def given_copy(step, b, h):
        return edge_copy(vec.at[step, h], step, b, h)

    def reply_copy(step, b, h):
        return edge_copy(reply.at[step, b, h], step, b, h)

    def down_copy(step, h):
        return pltpu.make_async_remote_copy(
            src_ref=vec.at[step, h], dst_ref=from_up.at[step, h], send_sem=down_send.at[step, h],
            recv_sem=down_recv.at[step, h], device_id={"shell": shell - 1}, device_id_type=MESH)

    def rise_copy(step, h):
        return pltpu.make_async_remote_copy(
            src_ref=lift.at[step, h], dst_ref=from_down.at[step, h], send_sem=rise_send.at[step, h],
            recv_sem=rise_recv.at[step, h], device_id={"shell": shell + 1}, device_id_type=MESH)

    barrier = pltpu.get_barrier_semaphore()
    for b in range(bits):
        pl.semaphore_signal(barrier, inc=1, device_id={"grp": partner[b]}, device_id_type=MESH)

    @pl.when(has_up)
    def _():
        pl.semaphore_signal(barrier, inc=1, device_id={"shell": shell + 1}, device_id_type=MESH)

    @pl.when(has_down)
    def _():
        pl.semaphore_signal(barrier, inc=1, device_id={"shell": shell - 1}, device_id_type=MESH)

    neighbours = bits + jnp.where(has_up, 1, 0) + jnp.where(has_down, 1, 0)

    def send_down(step, h):
        @pl.when(has_down)
        def _():
            down_copy(step, h).start()

    def send_vectors(step, h):
        for b in order:
            @pl.when(gives[b])
            def _():
                given_copy(step, b, h).start()

        send_down(step, h)

    def send_lift(step, h):
        @pl.when(has_up)
        def _():
            lift[step, h] = mm(up_t[...], vec[step, h]).astype(BF16)
            rise_copy(step, h).start()

    def send_reply(step, b, h):
        reply[step, b, h] = mm(full_t[b], vec[step, h]).astype(BF16)
        reply_copy(step, b, h).start()

    loads[1].wait()
    pl.semaphore_wait(barrier, neighbours)
    send_vectors(0, 0)

    for table in tables:
        table.wait()
    flips = [jnp.bitwise_xor(matchings[m, group], group) for m in range(matches)]
    loads[0].wait()
    for b in order:
        hits = [jnp.where(flips[m] == (1 << b), 1, 0) for m in range(matches)]
        which = jnp.minimum(sum(m * hits[m] for m in range(matches)), matches - 1)
        present = sum(hits)
        for i in range(parts):
            for j in range(parts):
                keep = (pair_mask[which * parts + i, 0, j] * present).astype(F32)
                keep = jnp.broadcast_to(keep, (BLK, BLK)).astype(BF16)
                block = pair_raw[which, pl.ds(i * BLK, BLK), pl.ds(j * BLK, BLK)]
                own[b, pl.ds(i * BLK, BLK), pl.ds(j * BLK, BLK)] = block * keep

        @pl.when(gives[b])
        def _():
            block_copy(b).start()

    for h in range(1, halves):
        loads[1 + h].wait()
        send_vectors(0, h)

    loads[1 + halves].wait()
    for i in range(parts):
        for j in range(parts):
            keep = jnp.broadcast_to(shell_mask[i, 0, j].astype(F32), (BLK, BLK)).astype(BF16)
            block = shell_raw[pl.ds(i * BLK, BLK), pl.ds(j * BLK, BLK)] * keep
            up[pl.ds(i * BLK, BLK), pl.ds(j * BLK, BLK)] = block
            up_t[pl.ds(j * BLK, BLK), pl.ds(i * BLK, BLK)] = block.T
    for h in range(halves):
        send_lift(0, h)

    loads[2 + halves].wait()
    for i in range(parts):
        for j in range(parts):
            here, there = pl.ds(i * BLK, BLK), pl.ds(j * BLK, BLK)
            sym[here, there] = (local_raw[here, there].astype(F32) + local_raw[there, here].T.astype(F32)).astype(BF16)

    def begin(step, h):
        v = vec[step, h]
        acc[step, h] = mm(sym[...], v) - spectrum_center * v.astype(F32)

    for h in range(halves):
        begin(0, h)

    def each_block(work):
        for i in range(parts):
            for j in range(parts):
                work(pl.ds(i * BLK, BLK), pl.ds(j * BLK, BLK))

    for b in range(bits):
        @pl.when(holds[b])
        def _():
            def turn(here, there):
                full_t[b, here, there] = own[b, there, here].T

            each_block(turn)

    for b in range(bits):
        @pl.when(holds[b])
        def _():
            def join(here, there):
                k_t = theirs[b, here, there].astype(F32) + full_t[b, here, there].astype(F32)
                full_t[b, here, there] = k_t.astype(BF16)

            block_copy(b).wait_recv()
            each_block(join)
            send_reply(0, b, 0)

    for h in range(1, halves):
        for b in order:
            @pl.when(holds[b])
            def _():
                send_reply(0, b, h)

    for b in range(bits):
        @pl.when(holds[b])
        def _():
            def turn_back(here, there):
                full[b, there, here] = full_t[b, here, there].T

            each_block(turn_back)

    def gather(step, h):
        @pl.when(has_up)
        def _():
            down_copy(step, h).wait_recv()
            acc[step, h] += mm(up[...], from_up[step, h])

        @pl.when(has_down)
        def _():
            rise_copy(step, h).wait_recv()
            acc[step, h] += from_down[step, h].astype(F32)

        for b in reversed(order):
            @pl.when(holds[b])
            def _():
                given_copy(step, b, h).wait_recv()
                acc[step, h] += mm(full[b], arrived[step, b, h])

        for b in reversed(order):
            @pl.when(gives[b])
            def _():
                reply_copy(step, b, h).wait_recv()
                acc[step, h] += arrived[step, b, h].astype(F32)

    for h in range(halves):
        gather(0, h)
        vec[1, h] = (acc[0, h] * (1.0 / spectrum_halfwidth)).astype(BF16)
        send_vectors(1, h)
        for b in order:
            @pl.when(holds[b])
            def _():
                send_reply(1, b, h)
        send_lift(1, h)
        begin(1, h)

    for h in range(halves):
        gather(1, h)
        y2 = acc[1, h] * (2.0 / spectrum_halfwidth) - vec[0, h].astype(F32)
        out[:, columns(h)] = y2.astype(BF16)

    for b in range(bits):
        @pl.when(gives[b])
        def _():
            block_copy(b).wait_send()
            for step in range(2):
                for h in range(halves):
                    given_copy(step, b, h).wait_send()

        @pl.when(holds[b])
        def _():
            for step in range(2):
                for h in range(halves):
                    reply_copy(step, b, h).wait_send()

    @pl.when(has_down)
    def _():
        for step in range(2):
            for h in range(halves):
                down_copy(step, h).wait_send()

    @pl.when(has_up)
    def _():
        for step in range(2):
            for h in range(halves):
                rise_copy(step, h).wait_send()


def on_device(bits, shells, vectors, local_block, pair_blocks, pair_masks, shell_block, shell_mask, matchings):
    rows, width = vectors.shape[2:]
    matches = pair_blocks.shape[2]
    halves = width // LANES
    parts = pair_masks.shape[-1]
    pair_masks = pair_masks.reshape(matches * parts, 1, parts)
    shell_mask = shell_mask.reshape(parts, 1, parts)
    square = (rows, rows)
    tall = (halves, rows, LANES)
    out = pl.pallas_call(
        functools.partial(filter_kernel, bits, shells),
        out_shape=jax.ShapeDtypeStruct((rows, width), BF16),
        in_specs=[pl.BlockSpec(memory_space=pltpu.HBM)] * 7,
        out_specs=pl.BlockSpec(memory_space=pltpu.VMEM),
        scratch_shapes=[
            pltpu.SMEM(pair_masks.shape, jnp.int32),
            pltpu.SMEM(shell_mask.shape, jnp.int32),
            pltpu.SMEM(matchings.shape, jnp.int32),
            pltpu.VMEM((2,) + tall, BF16),
            pltpu.VMEM(square, BF16),
            pltpu.VMEM((matches,) + square, BF16),
            pltpu.VMEM(square, BF16),
            pltpu.VMEM((bits,) + square, BF16),
            pltpu.VMEM((bits,) + square, BF16),
            pltpu.VMEM((bits,) + square, BF16),
            pltpu.VMEM((bits,) + square, BF16),
            pltpu.VMEM(square, BF16),
            pltpu.VMEM(square, BF16),
            pltpu.VMEM(square, BF16),
            pltpu.VMEM((2, bits) + tall, BF16),
            pltpu.VMEM((2, bits) + tall, BF16),
            pltpu.VMEM((2,) + tall, BF16),
            pltpu.VMEM((2,) + tall, BF16),
            pltpu.VMEM((2,) + tall, BF16),
            pltpu.VMEM((2,) + tall, F32),
            pltpu.SemaphoreType.DMA((6 + halves,)),
            pltpu.SemaphoreType.DMA((bits,)),
            pltpu.SemaphoreType.DMA((bits,)),
            pltpu.SemaphoreType.DMA((2, bits, halves)),
            pltpu.SemaphoreType.DMA((2, bits, halves)),
            pltpu.SemaphoreType.DMA((2, halves)),
            pltpu.SemaphoreType.DMA((2, halves)),
            pltpu.SemaphoreType.DMA((2, halves)),
            pltpu.SemaphoreType.DMA((2, halves)),
        ],
        compiler_params=pltpu.CompilerParams(
            collective_id=0, has_side_effects=True, vmem_limit_bytes=40 * 1024 * 1024
        ),
    )(*[
        pltpu.with_memory_space_constraint(x, pltpu.HBM)
        for x in (
            vectors[0, 0],
            local_block[0, 0],
            pair_blocks[0, 0],
            shell_block[0, 0],
            pair_masks,
            shell_mask,
            matchings,
        )
    ])
    return out[None, None]


def solution(mesh):
    sizes = dict(mesh.shape)
    bits = sizes["grp"].bit_length() - 1
    in_specs = (
        P("grp", "shell", None, None),
        P("grp", "shell", None, None),
        P("grp", "shell", None, None, None),
        P("grp", "shell", None, None, None),
        P("grp", "shell", None, None),
        P("grp", "shell", None, None),
        P(),
    )
    out_specs = P("grp", "shell", None, None)
    return jax.shard_map(
        functools.partial(on_device, bits, sizes["shell"]),
        mesh=mesh, in_specs=in_specs, out_specs=out_specs, check_vma=False,
    )
```

```python
import functools

import jax
import jax.numpy as jnp
from jax import lax
from jax.experimental import pallas as pl
from jax.experimental.pallas import tpu as pltpu
from jax.sharding import PartitionSpec as P

BLK = 128
LANES = 128

spectrum_center = 1.0
spectrum_halfwidth = 6.0

MESH = pl.DeviceIdType.MESH
F32 = jnp.float32
BF16 = jnp.bfloat16


def mm(a, b):
    return jnp.dot(a, b, preferred_element_type=F32)


def filter_kernel(
    bits,
    shells,
    vec_hbm,
    local_hbm,
    pair_hbm,
    shell_hbm,
    pair_mask_hbm,
    shell_mask_hbm,
    matchings_hbm,
    out,
    pair_mask,
    shell_mask,
    matchings,
    vec,
    local_raw,
    pair_raw,
    shell_raw,
    own,
    theirs,
    full,
    full_t,
    sym,
    up,
    up_t,
    reply,
    arrived,
    lift,
    from_up,
    from_down,
    acc,
    load_sem,
    block_send,
    block_recv,
    edge_send,
    edge_recv,
    down_send,
    down_recv,
    rise_send,
    rise_recv,
):
    halves = vec.shape[1]
    rows = vec.shape[2]
    parts = rows // BLK
    matches = pair_raw.shape[0]
    group = lax.axis_index("grp")
    shell = lax.axis_index("shell")
    has_up = shell < shells - 1
    has_down = shell > 0
    order = list(reversed(range(bits)))

    def digit(b):
        return (group // (1 << b)) % 2

    partner = [group + (1 << b) - 2 * (1 << b) * digit(b) for b in range(bits)]
    role = [(digit(b) + (digit((b + 1) % bits) if bits > 1 else 0) + shell) % 2 for b in range(bits)]
    holds = [role[b] == 1 for b in range(bits)]
    gives = [role[b] == 0 for b in range(bits)]

    columns = lambda h: pl.ds(h * LANES, LANES)
    loads = [pltpu.make_async_copy(pair_hbm, pair_raw, load_sem.at[0])]
    for h in range(halves):
        loads.append(pltpu.make_async_copy(vec_hbm.at[:, columns(h)], vec.at[0, h], load_sem.at[1 + h]))
    loads.append(pltpu.make_async_copy(shell_hbm, shell_raw, load_sem.at[1 + halves]))
    loads.append(pltpu.make_async_copy(local_hbm, local_raw, load_sem.at[2 + halves]))
    tables = [
        pltpu.make_async_copy(matchings_hbm, matchings, load_sem.at[3 + halves]),
        pltpu.make_async_copy(pair_mask_hbm, pair_mask, load_sem.at[4 + halves]),
        pltpu.make_async_copy(shell_mask_hbm, shell_mask, load_sem.at[5 + halves]),
    ]
    for load in tables + loads:
        load.start()

    def block_copy(b):
        return pltpu.make_async_remote_copy(
            src_ref=own.at[b], dst_ref=theirs.at[b], send_sem=block_send.at[b], recv_sem=block_recv.at[b],
            device_id={"grp": partner[b]}, device_id_type=MESH)

    def edge_copy(source, step, b, h):
        return pltpu.make_async_remote_copy(
            src_ref=source, dst_ref=arrived.at[step, b, h], send_sem=edge_send.at[step, b, h],
            recv_sem=edge_recv.at[step, b, h], device_id={"grp": partner[b]}, device_id_type=MESH)

    def given_copy(step, b, h):
        return edge_copy(vec.at[step, h], step, b, h)

    def reply_copy(step, b, h):
        return edge_copy(reply.at[step, b, h], step, b, h)

    def down_copy(step, h):
        return pltpu.make_async_remote_copy(
            src_ref=vec.at[step, h], dst_ref=from_up.at[step, h], send_sem=down_send.at[step, h],
            recv_sem=down_recv.at[step, h], device_id={"shell": shell - 1}, device_id_type=MESH)

    def rise_copy(step, h):
        return pltpu.make_async_remote_copy(
            src_ref=lift.at[step, h], dst_ref=from_down.at[step, h], send_sem=rise_send.at[step, h],
            recv_sem=rise_recv.at[step, h], device_id={"shell": shell + 1}, device_id_type=MESH)

    barrier = pltpu.get_barrier_semaphore()
    for b in range(bits):
        pl.semaphore_signal(barrier, inc=1, device_id={"grp": partner[b]}, device_id_type=MESH)

    @pl.when(has_up)
    def _():
        pl.semaphore_signal(barrier, inc=1, device_id={"shell": shell + 1}, device_id_type=MESH)

    @pl.when(has_down)
    def _():
        pl.semaphore_signal(barrier, inc=1, device_id={"shell": shell - 1}, device_id_type=MESH)

    neighbours = bits + jnp.where(has_up, 1, 0) + jnp.where(has_down, 1, 0)

    def send_down(step, h):
        @pl.when(has_down)
        def _():
            down_copy(step, h).start()

    def send_vectors(step, h):
        for b in order:
            @pl.when(gives[b])
            def _():
                given_copy(step, b, h).start()

        send_down(step, h)

    def send_lift(step, h):
        @pl.when(has_up)
        def _():
            lift[step, h] = mm(up_t[...], vec[step, h]).astype(BF16)
            rise_copy(step, h).start()

    def send_reply(step, b, h):
        reply[step, b, h] = mm(full_t[b], vec[step, h]).astype(BF16)
        reply_copy(step, b, h).start()

    for table in tables:
        table.wait()
    flips = [jnp.bitwise_xor(matchings[m, group], group) for m in range(matches)]
    loads[0].wait()
    for at, b in enumerate(order):
        hits = [jnp.where(flips[m] == (1 << b), 1, 0) for m in range(matches)]
        which = jnp.minimum(sum(m * hits[m] for m in range(matches)), matches - 1)
        present = sum(hits)
        for i in range(parts):
            for j in range(parts):
                keep = (pair_mask[which * parts + i, 0, j] * present).astype(F32)
                keep = jnp.broadcast_to(keep, (BLK, BLK)).astype(BF16)
                block = pair_raw[which, pl.ds(i * BLK, BLK), pl.ds(j * BLK, BLK)]
                own[b, pl.ds(i * BLK, BLK), pl.ds(j * BLK, BLK)] = block * keep

        if at == 0:
            pl.semaphore_wait(barrier, neighbours)

        @pl.when(gives[b])
        def _():
            block_copy(b).start()

    for h in range(halves):
        loads[1 + h].wait()
        send_down(0, h)

    loads[1 + halves].wait()
    for i in range(parts):
        for j in range(parts):
            keep = jnp.broadcast_to(shell_mask[i, 0, j].astype(F32), (BLK, BLK)).astype(BF16)
            block = shell_raw[pl.ds(i * BLK, BLK), pl.ds(j * BLK, BLK)] * keep
            up[pl.ds(i * BLK, BLK), pl.ds(j * BLK, BLK)] = block
            up_t[pl.ds(j * BLK, BLK), pl.ds(i * BLK, BLK)] = block.T
    for h in range(halves):
        send_lift(0, h)

    loads[2 + halves].wait()
    for i in range(parts):
        for j in range(parts):
            here, there = pl.ds(i * BLK, BLK), pl.ds(j * BLK, BLK)
            sym[here, there] = (local_raw[here, there].astype(F32) + local_raw[there, here].T.astype(F32)).astype(BF16)

    def begin(step, h):
        v = vec[step, h]
        acc[step, h] = mm(sym[...], v) - spectrum_center * v.astype(F32)

    for h in range(halves):
        begin(0, h)

    def each_block(work):
        for i in range(parts):
            for j in range(parts):
                work(pl.ds(i * BLK, BLK), pl.ds(j * BLK, BLK))

    for b in range(bits):
        @pl.when(holds[b])
        def _():
            def turn(here, there):
                full_t[b, here, there] = own[b, there, here].T

            each_block(turn)

    for b in range(bits):
        @pl.when(holds[b])
        def _():
            def join(here, there):
                k_t = theirs[b, here, there].astype(F32) + full_t[b, here, there].astype(F32)
                full_t[b, here, there] = k_t.astype(BF16)

            block_copy(b).wait_recv()
            each_block(join)
            send_reply(0, b, 0)

        if b == 0:
            for c in range(bits):
                @pl.when(gives[c])
                def _():
                    block_copy(c).wait_send()
                    given_copy(0, c, 0).start()

    for h in range(1, halves):
        for b in range(bits):
            @pl.when(gives[b])
            def _():
                given_copy(0, b, h - 1).wait_send()
                given_copy(0, b, h).start()

        for b in order:
            @pl.when(holds[b])
            def _():
                send_reply(0, b, h)

    for b in range(bits):
        @pl.when(holds[b])
        def _():
            def turn_back(here, there):
                full[b, there, here] = full_t[b, here, there].T

            each_block(turn_back)

    def gather(step, h):
        @pl.when(has_up)
        def _():
            down_copy(step, h).wait_recv()
            acc[step, h] += mm(up[...], from_up[step, h])

        @pl.when(has_down)
        def _():
            rise_copy(step, h).wait_recv()
            acc[step, h] += from_down[step, h].astype(F32)

        for b in reversed(order):
            @pl.when(holds[b])
            def _():
                given_copy(step, b, h).wait_recv()
                acc[step, h] += mm(full[b], arrived[step, b, h])

        for b in reversed(order):
            @pl.when(gives[b])
            def _():
                reply_copy(step, b, h).wait_recv()
                acc[step, h] += arrived[step, b, h].astype(F32)

    for h in range(halves):
        gather(0, h)
        vec[1, h] = (acc[0, h] * (1.0 / spectrum_halfwidth)).astype(BF16)
        send_vectors(1, h)
        for b in order:
            @pl.when(holds[b])
            def _():
                send_reply(1, b, h)
        send_lift(1, h)
        begin(1, h)

    for h in range(halves):
        gather(1, h)
        y2 = acc[1, h] * (2.0 / spectrum_halfwidth) - vec[0, h].astype(F32)
        out[:, columns(h)] = y2.astype(BF16)

    for b in range(bits):
        @pl.when(gives[b])
        def _():
            given_copy(0, b, halves - 1).wait_send()
            for h in range(halves):
                given_copy(1, b, h).wait_send()

        @pl.when(holds[b])
        def _():
            for step in range(2):
                for h in range(halves):
                    reply_copy(step, b, h).wait_send()

    @pl.when(has_down)
    def _():
        for step in range(2):
            for h in range(halves):
                down_copy(step, h).wait_send()

    @pl.when(has_up)
    def _():
        for step in range(2):
            for h in range(halves):
                rise_copy(step, h).wait_send()


def on_device(bits, shells, vectors, local_block, pair_blocks, pair_masks, shell_block, shell_mask, matchings):
    rows, width = vectors.shape[2:]
    matches = pair_blocks.shape[2]
    halves = width // LANES
    parts = pair_masks.shape[-1]
    pair_masks = pair_masks.reshape(matches * parts, 1, parts)
    shell_mask = shell_mask.reshape(parts, 1, parts)
    square = (rows, rows)
    tall = (halves, rows, LANES)
    out = pl.pallas_call(
        functools.partial(filter_kernel, bits, shells),
        out_shape=jax.ShapeDtypeStruct((rows, width), BF16),
        in_specs=[pl.BlockSpec(memory_space=pltpu.HBM)] * 7,
        out_specs=pl.BlockSpec(memory_space=pltpu.VMEM),
        scratch_shapes=[
            pltpu.SMEM(pair_masks.shape, jnp.int32),
            pltpu.SMEM(shell_mask.shape, jnp.int32),
            pltpu.SMEM(matchings.shape, jnp.int32),
            pltpu.VMEM((2,) + tall, BF16),
            pltpu.VMEM(square, BF16),
            pltpu.VMEM((matches,) + square, BF16),
            pltpu.VMEM(square, BF16),
            pltpu.VMEM((bits,) + square, BF16),
            pltpu.VMEM((bits,) + square, BF16),
            pltpu.VMEM((bits,) + square, BF16),
            pltpu.VMEM((bits,) + square, BF16),
            pltpu.VMEM(square, BF16),
            pltpu.VMEM(square, BF16),
            pltpu.VMEM(square, BF16),
            pltpu.VMEM((2, bits) + tall, BF16),
            pltpu.VMEM((2, bits) + tall, BF16),
            pltpu.VMEM((2,) + tall, BF16),
            pltpu.VMEM((2,) + tall, BF16),
            pltpu.VMEM((2,) + tall, BF16),
            pltpu.VMEM((2,) + tall, F32),
            pltpu.SemaphoreType.DMA((6 + halves,)),
            pltpu.SemaphoreType.DMA((bits,)),
            pltpu.SemaphoreType.DMA((bits,)),
            pltpu.SemaphoreType.DMA((2, bits, halves)),
            pltpu.SemaphoreType.DMA((2, bits, halves)),
            pltpu.SemaphoreType.DMA((2, halves)),
            pltpu.SemaphoreType.DMA((2, halves)),
            pltpu.SemaphoreType.DMA((2, halves)),
            pltpu.SemaphoreType.DMA((2, halves)),
        ],
        compiler_params=pltpu.CompilerParams(
            collective_id=0, has_side_effects=True, vmem_limit_bytes=40 * 1024 * 1024
        ),
    )(*[
        pltpu.with_memory_space_constraint(x, pltpu.HBM)
        for x in (
            vectors[0, 0],
            local_block[0, 0],
            pair_blocks[0, 0],
            shell_block[0, 0],
            pair_masks,
            shell_mask,
            matchings,
        )
    ])
    return out[None, None]


def solution(mesh):
    sizes = dict(mesh.shape)
    bits = sizes["grp"].bit_length() - 1
    in_specs = (
        P("grp", "shell", None, None),
        P("grp", "shell", None, None),
        P("grp", "shell", None, None, None),
        P("grp", "shell", None, None, None),
        P("grp", "shell", None, None),
        P("grp", "shell", None, None),
        P(),
    )
    out_specs = P("grp", "shell", None, None)
    return jax.shard_map(
        functools.partial(on_device, bits, sizes["shell"]),
        mesh=mesh, in_specs=in_specs, out_specs=out_specs, check_vma=False,
    )
```

```python
import functools

import jax
import jax.numpy as jnp
from jax import lax
from jax.experimental import pallas as pl
from jax.experimental.pallas import tpu as pltpu
from jax.sharding import PartitionSpec as P

BLK = 128
LANES = 128

spectrum_center = 1.0
spectrum_halfwidth = 6.0

MESH = pl.DeviceIdType.MESH
F32 = jnp.float32
BF16 = jnp.bfloat16


def mm(a, b):
    return jnp.dot(a, b, preferred_element_type=F32)


def mm_t(a, b):
    return lax.dot_general(a, b, (((1,), (1,)), ((), ())), preferred_element_type=F32)


def turned(x):
    return x.astype(F32).T


def filter_kernel(
    bits,
    shells,
    vec_hbm,
    local_hbm,
    pair_hbm,
    shell_hbm,
    pair_mask_hbm,
    shell_mask_hbm,
    matchings_hbm,
    out,
    pair_mask,
    shell_mask,
    matchings,
    vec_raw,
    vec,
    local_raw,
    pair_raw,
    shell_raw,
    own,
    theirs,
    up,
    partial,
    reply,
    arrived,
    lift,
    from_up,
    from_down,
    acc,
    load_sem,
    block_send,
    block_recv,
    edge_send,
    edge_recv,
    down_send,
    down_recv,
    rise_send,
    rise_recv,
):
    halves = vec.shape[1] // LANES
    rows = vec.shape[2]
    parts = rows // BLK
    matches = pair_raw.shape[0]
    group = lax.axis_index("grp")
    shell = lax.axis_index("shell")
    has_up = shell < shells - 1
    has_down = shell > 0
    order = list(reversed(range(bits)))

    def digit(b):
        return (group // (1 << b)) % 2

    partner = [group + (1 << b) - 2 * (1 << b) * digit(b) for b in range(bits)]
    other = [bits - 1] + [(b + 1) % bits for b in range(1, bits)]
    role = [(digit(b) + (digit(other[b]) if bits > 1 else 0) + (b == 0) + shell) % 2 for b in range(bits)]
    holds = [role[b] == 1 for b in range(bits)]
    gives = [role[b] == 0 for b in range(bits)]

    columns = lambda h: pl.ds(h * LANES, LANES)
    loads = [pltpu.make_async_copy(pair_hbm, pair_raw, load_sem.at[0])]
    for h in range(halves):
        loads.append(pltpu.make_async_copy(vec_hbm.at[:, columns(h)], vec_raw.at[:, columns(h)], load_sem.at[1 + h]))
    loads.append(pltpu.make_async_copy(shell_hbm, shell_raw, load_sem.at[1 + halves]))
    loads.append(pltpu.make_async_copy(local_hbm, local_raw, load_sem.at[2 + halves]))
    tables = [
        pltpu.make_async_copy(matchings_hbm, matchings, load_sem.at[3 + halves]),
        pltpu.make_async_copy(pair_mask_hbm, pair_mask, load_sem.at[4 + halves]),
        pltpu.make_async_copy(shell_mask_hbm, shell_mask, load_sem.at[5 + halves]),
    ]
    for load in tables + loads:
        load.start()

    def block_copy(b):
        return pltpu.make_async_remote_copy(
            src_ref=own.at[b], dst_ref=theirs.at[b], send_sem=block_send.at[b], recv_sem=block_recv.at[b],
            device_id={"grp": partner[b]}, device_id_type=MESH)

    def edge_copy(source, step, b, h):
        return pltpu.make_async_remote_copy(
            src_ref=source, dst_ref=arrived.at[step, b, columns(h)], send_sem=edge_send.at[step, b, h],
            recv_sem=edge_recv.at[step, b, h], device_id={"grp": partner[b]}, device_id_type=MESH)

    def given_copy(step, b, h):
        return edge_copy(vec.at[step, columns(h)], step, b, h)

    def reply_copy(step, b, h):
        return edge_copy(reply.at[step, b, columns(h)], step, b, h)

    def down_copy(step, h):
        return pltpu.make_async_remote_copy(
            src_ref=vec.at[step, columns(h)], dst_ref=from_up.at[step, columns(h)], send_sem=down_send.at[step, h],
            recv_sem=down_recv.at[step, h], device_id={"shell": shell - 1}, device_id_type=MESH)

    def rise_copy(step, h):
        return pltpu.make_async_remote_copy(
            src_ref=lift.at[step, columns(h)], dst_ref=from_down.at[step, columns(h)], send_sem=rise_send.at[step, h],
            recv_sem=rise_recv.at[step, h], device_id={"shell": shell + 1}, device_id_type=MESH)

    barrier = pltpu.get_barrier_semaphore()
    for b in range(bits):
        pl.semaphore_signal(barrier, inc=1, device_id={"grp": partner[b]}, device_id_type=MESH)

    @pl.when(has_up)
    def _():
        pl.semaphore_signal(barrier, inc=1, device_id={"shell": shell + 1}, device_id_type=MESH)

    @pl.when(has_down)
    def _():
        pl.semaphore_signal(barrier, inc=1, device_id={"shell": shell - 1}, device_id_type=MESH)

    neighbours = bits + jnp.where(has_up, 1, 0) + jnp.where(has_down, 1, 0)

    for table in tables:
        table.wait()
    flips = [jnp.bitwise_xor(matchings[m, group], group) for m in range(matches)]
    loads[0].wait()
    for at, b in enumerate(order):
        hits = [jnp.where(flips[m] == (1 << b), 1, 0) for m in range(matches)]
        which = jnp.minimum(sum(m * hits[m] for m in range(matches)), matches - 1)
        present = sum(hits)
        for i in range(parts):
            for j in range(parts):
                keep = (pair_mask[which * parts + i, 0, j] * present).astype(F32)
                block = pair_raw[which, pl.ds(i * BLK, BLK), pl.ds(j * BLK, BLK)]
                own[b, pl.ds(i * BLK, BLK), pl.ds(j * BLK, BLK)] = (block.astype(F32) * keep).astype(BF16)
        if at == 0:
            pl.semaphore_wait(barrier, neighbours)

        @pl.when(gives[b])
        def _():
            block_copy(b).start()

    def send_vectors(step, h):
        for b in order:
            @pl.when(gives[b])
            def _():
                given_copy(step, b, h).start()

        @pl.when(has_down)
        def _():
            down_copy(step, h).start()

    def start_lift(step, h):
        @pl.when(has_up)
        def _():
            rise_copy(step, h).start()

    def start_replies(step, h):
        for b in order:
            @pl.when(holds[b])
            def _():
                reply_copy(step, b, h).start()

    for h in range(halves):
        loads[1 + h].wait()
        for i in range(parts):
            here = pl.ds(i * BLK, BLK)
            vec[0, columns(h), here] = turned(vec_raw[here, columns(h)]).astype(BF16)
        send_vectors(0, h)

    for b in range(bits):
        @pl.when(holds[b])
        def _():
            partial[b] = mm(vec[0], own[b])

    loads[1 + halves].wait()
    for i in range(parts):
        for j in range(parts):
            keep = shell_mask[i, 0, j].astype(F32)
            block = shell_raw[pl.ds(i * BLK, BLK), pl.ds(j * BLK, BLK)].astype(F32) * keep
            up[pl.ds(i * BLK, BLK), pl.ds(j * BLK, BLK)] = block.astype(BF16)

    @pl.when(has_up)
    def _():
        lift[0] = mm(vec[0], up[...]).astype(BF16)

    for h in range(halves):
        start_lift(0, h)

    loads[2 + halves].wait()

    def begin(step, part):
        v = vec[step, part]
        acc[step, part] = mm_t(v, local_raw[...]) + mm(v, local_raw[...]) - spectrum_center * v.astype(F32)

    begin(0, pl.ds(0, halves * LANES))

    for b in range(bits):
        @pl.when(holds[b])
        def _():
            block_copy(b).wait_recv()
            reply[0, b] = (partial[b] + mm_t(vec[0], theirs[b])).astype(BF16)
            reply_copy(0, b, 0).start()

    for h in range(1, halves):
        start_replies(0, h)

    def gather(step, h):
        part = columns(h)

        @pl.when(has_up)
        def _():
            down_copy(step, h).wait_recv()
            acc[step, part] += mm_t(from_up[step, part], up[...])

        @pl.when(has_down)
        def _():
            rise_copy(step, h).wait_recv()
            acc[step, part] += from_down[step, part].astype(F32)

        for b in range(bits):
            @pl.when(holds[b])
            def _():
                given_copy(step, b, h).wait_recv()
                x = arrived[step, b, part]
                acc[step, part] += mm_t(x, own[b]) + mm(x, theirs[b])

        for b in range(bits):
            @pl.when(gives[b])
            def _():
                reply_copy(step, b, h).wait_recv()
                acc[step, part] += arrived[step, b, part].astype(F32)

    for h in range(halves):
        part = columns(h)
        gather(0, h)
        vec[1, part] = (acc[0, part] * (1.0 / spectrum_halfwidth)).astype(BF16)
        send_vectors(1, h)
        for b in order:
            @pl.when(holds[b])
            def _():
                v = vec[1, part]
                reply[1, b, part] = (mm(v, own[b]) + mm_t(v, theirs[b])).astype(BF16)
                reply_copy(1, b, h).start()

        @pl.when(has_up)
        def _():
            lift[1, part] = mm(vec[1, part], up[...]).astype(BF16)

        start_lift(1, h)
        begin(1, part)

    for h in range(halves):
        gather(1, h)
        for i in range(parts):
            here = pl.ds(i * BLK, BLK)
            y2 = (acc[1, columns(h), here] * (2.0 / spectrum_halfwidth)).T - vec_raw[here, columns(h)].astype(F32)
            out[here, columns(h)] = y2.astype(BF16)

    for b in range(bits):
        @pl.when(gives[b])
        def _():
            block_copy(b).wait_send()
            for step in range(2):
                for h in range(halves):
                    given_copy(step, b, h).wait_send()

        @pl.when(holds[b])
        def _():
            for step in range(2):
                for h in range(halves):
                    reply_copy(step, b, h).wait_send()

    @pl.when(has_down)
    def _():
        for step in range(2):
            for h in range(halves):
                down_copy(step, h).wait_send()

    @pl.when(has_up)
    def _():
        for step in range(2):
            for h in range(halves):
                rise_copy(step, h).wait_send()


def on_device(bits, shells, vectors, local_block, pair_blocks, pair_masks, shell_block, shell_mask, matchings):
    rows, width = vectors.shape[2:]
    matches = pair_blocks.shape[2]
    halves = width // LANES
    parts = pair_masks.shape[-1]
    pair_masks = pair_masks.reshape(matches * parts, 1, parts)
    shell_mask = shell_mask.reshape(parts, 1, parts)
    square = (rows, rows)
    wide = (width, rows)
    out = pl.pallas_call(
        functools.partial(filter_kernel, bits, shells),
        out_shape=jax.ShapeDtypeStruct((rows, width), BF16),
        in_specs=[pl.BlockSpec(memory_space=pltpu.HBM)] * 7,
        out_specs=pl.BlockSpec(memory_space=pltpu.VMEM),
        scratch_shapes=[
            pltpu.SMEM(pair_masks.shape, jnp.int32),
            pltpu.SMEM(shell_mask.shape, jnp.int32),
            pltpu.SMEM(matchings.shape, jnp.int32),
            pltpu.VMEM((rows, width), BF16),
            pltpu.VMEM((2,) + wide, BF16),
            pltpu.VMEM(square, BF16),
            pltpu.VMEM((matches,) + square, BF16),
            pltpu.VMEM(square, BF16),
            pltpu.VMEM((bits,) + square, BF16),
            pltpu.VMEM((bits,) + square, BF16),
            pltpu.VMEM(square, BF16),
            pltpu.VMEM((bits,) + wide, F32),
            pltpu.VMEM((2, bits) + wide, BF16),
            pltpu.VMEM((2, bits) + wide, BF16),
            pltpu.VMEM((2,) + wide, BF16),
            pltpu.VMEM((2,) + wide, BF16),
            pltpu.VMEM((2,) + wide, BF16),
            pltpu.VMEM((2,) + wide, F32),
            pltpu.SemaphoreType.DMA((6 + halves,)),
            pltpu.SemaphoreType.DMA((bits,)),
            pltpu.SemaphoreType.DMA((bits,)),
            pltpu.SemaphoreType.DMA((2, bits, halves)),
            pltpu.SemaphoreType.DMA((2, bits, halves)),
            pltpu.SemaphoreType.DMA((2, halves)),
            pltpu.SemaphoreType.DMA((2, halves)),
            pltpu.SemaphoreType.DMA((2, halves)),
            pltpu.SemaphoreType.DMA((2, halves)),
        ],
        compiler_params=pltpu.CompilerParams(
            collective_id=0, has_side_effects=True, vmem_limit_bytes=40 * 1024 * 1024
        ),
    )(*[
        pltpu.with_memory_space_constraint(x, pltpu.HBM)
        for x in (
            vectors[0, 0],
            local_block[0, 0],
            pair_blocks[0, 0],
            shell_block[0, 0],
            pair_masks,
            shell_mask,
            matchings,
        )
    ])
    return out[None, None]


def solution(mesh):
    sizes = dict(mesh.shape)
    bits = sizes["grp"].bit_length() - 1
    in_specs = (
        P("grp", "shell", None, None),
        P("grp", "shell", None, None),
        P("grp", "shell", None, None, None),
        P("grp", "shell", None, None, None),
        P("grp", "shell", None, None),
        P("grp", "shell", None, None),
        P(),
    )
    out_specs = P("grp", "shell", None, None)
    return jax.shard_map(
        functools.partial(on_device, bits, sizes["shell"]),
        mesh=mesh, in_specs=in_specs, out_specs=out_specs, check_vma=False,
    )
```

```python
import functools

import jax
import jax.numpy as jnp
from jax import lax
from jax.experimental import pallas as pl
from jax.experimental.pallas import tpu as pltpu
from jax.sharding import PartitionSpec as P

BLK = 128
LANES = 128

spectrum_center = 1.0
spectrum_halfwidth = 6.0

MESH = pl.DeviceIdType.MESH
F32 = jnp.float32
BF16 = jnp.bfloat16


def mm(a, b):
    return jnp.dot(a, b, preferred_element_type=F32)


def mm_t(a, b):
    return lax.dot_general(a, b, (((1,), (1,)), ((), ())), preferred_element_type=F32)


def turned(x):
    return x.astype(F32).T


def filter_kernel(
    bits,
    shells,
    vec_hbm,
    local_hbm,
    pair_hbm,
    shell_hbm,
    pair_mask_hbm,
    shell_mask_hbm,
    matchings_hbm,
    out,
    pair_mask,
    shell_mask,
    matchings,
    vec_raw,
    vec,
    local_raw,
    pair_raw,
    shell_raw,
    own,
    theirs,
    up,
    partial,
    reply,
    arrived,
    lift,
    from_up,
    from_down,
    acc,
    load_sem,
    block_send,
    block_recv,
    edge_send,
    edge_recv,
    down_send,
    down_recv,
    rise_send,
    rise_recv,
):
    halves = vec.shape[1] // LANES
    rows = vec.shape[2]
    parts = rows // BLK
    matches = pair_raw.shape[0]
    group = lax.axis_index("grp")
    shell = lax.axis_index("shell")
    has_up = shell < shells - 1
    has_down = shell > 0
    order = list(reversed(range(bits)))

    def digit(b):
        return (group // (1 << b)) % 2

    partner = [group + (1 << b) - 2 * (1 << b) * digit(b) for b in range(bits)]
    other = [bits - 1] + [(b + 1) % bits for b in range(1, bits)]
    role = [(digit(b) + (digit(other[b]) if bits > 1 else 0) + (b == 0) + shell) % 2 for b in range(bits)]
    holds = [role[b] == 1 for b in range(bits)]
    gives = [role[b] == 0 for b in range(bits)]

    columns = lambda h: pl.ds(h * LANES, LANES)
    loads = [pltpu.make_async_copy(pair_hbm, pair_raw, load_sem.at[0])]
    for h in range(halves):
        loads.append(pltpu.make_async_copy(vec_hbm.at[:, columns(h)], vec_raw.at[:, columns(h)], load_sem.at[1 + h]))
    loads.append(pltpu.make_async_copy(shell_hbm, shell_raw, load_sem.at[1 + halves]))
    loads.append(pltpu.make_async_copy(local_hbm, local_raw, load_sem.at[2 + halves]))
    tables = [
        pltpu.make_async_copy(matchings_hbm, matchings, load_sem.at[3 + halves]),
        pltpu.make_async_copy(pair_mask_hbm, pair_mask, load_sem.at[4 + halves]),
        pltpu.make_async_copy(shell_mask_hbm, shell_mask, load_sem.at[5 + halves]),
    ]
    for load in tables + loads:
        load.start()

    def block_copy(b):
        return pltpu.make_async_remote_copy(
            src_ref=own.at[b], dst_ref=theirs.at[b], send_sem=block_send.at[b], recv_sem=block_recv.at[b],
            device_id={"grp": partner[b]}, device_id_type=MESH)

    def edge_copy(source, step, b, h):
        return pltpu.make_async_remote_copy(
            src_ref=source, dst_ref=arrived.at[step, b, columns(h)], send_sem=edge_send.at[step, b, h],
            recv_sem=edge_recv.at[step, b, h], device_id={"grp": partner[b]}, device_id_type=MESH)

    def given_copy(step, b, h):
        return edge_copy(vec.at[step, columns(h)], step, b, h)

    def reply_copy(step, b, h):
        return edge_copy(reply.at[step, b, columns(h)], step, b, h)

    def down_copy(step, h):
        return pltpu.make_async_remote_copy(
            src_ref=vec.at[step, columns(h)], dst_ref=from_up.at[step, columns(h)], send_sem=down_send.at[step, h],
            recv_sem=down_recv.at[step, h], device_id={"shell": shell - 1}, device_id_type=MESH)

    def rise_copy(step, h):
        return pltpu.make_async_remote_copy(
            src_ref=lift.at[step, columns(h)], dst_ref=from_down.at[step, columns(h)], send_sem=rise_send.at[step, h],
            recv_sem=rise_recv.at[step, h], device_id={"shell": shell + 1}, device_id_type=MESH)

    barrier = pltpu.get_barrier_semaphore()
    for b in range(bits):
        pl.semaphore_signal(barrier, inc=1, device_id={"grp": partner[b]}, device_id_type=MESH)

    @pl.when(has_up)
    def _():
        pl.semaphore_signal(barrier, inc=1, device_id={"shell": shell + 1}, device_id_type=MESH)

    @pl.when(has_down)
    def _():
        pl.semaphore_signal(barrier, inc=1, device_id={"shell": shell - 1}, device_id_type=MESH)

    neighbours = bits + jnp.where(has_up, 1, 0) + jnp.where(has_down, 1, 0)

    for table in tables:
        table.wait()
    flips = [jnp.bitwise_xor(matchings[m, group], group) for m in range(matches)]
    loads[0].wait()
    for at, b in enumerate(order):
        hits = [jnp.where(flips[m] == (1 << b), 1, 0) for m in range(matches)]
        which = jnp.minimum(sum(m * hits[m] for m in range(matches)), matches - 1)
        present = sum(hits)
        for i in range(parts):
            for j in range(parts):
                keep = (pair_mask[which * parts + i, 0, j] * present).astype(F32)
                block = pair_raw[which, pl.ds(i * BLK, BLK), pl.ds(j * BLK, BLK)]
                own[b, pl.ds(i * BLK, BLK), pl.ds(j * BLK, BLK)] = (block.astype(F32) * keep).astype(BF16)
        if at == 0:
            pl.semaphore_wait(barrier, neighbours)

        @pl.when(gives[b])
        def _():
            block_copy(b).start()

    def send_down(step, h):
        @pl.when(has_down)
        def _():
            down_copy(step, h).start()

    def send_vectors(step, h):
        for b in order:
            @pl.when(gives[b])
            def _():
                given_copy(step, b, h).start()

        send_down(step, h)

    def start_lift(step, h):
        @pl.when(has_up)
        def _():
            rise_copy(step, h).start()

    for h in range(halves):
        loads[1 + h].wait()
        for i in range(parts):
            here = pl.ds(i * BLK, BLK)
            vec[0, columns(h), here] = turned(vec_raw[here, columns(h)]).astype(BF16)
        send_down(0, h)

    for b in range(bits):
        @pl.when(holds[b])
        def _():
            partial[b] = mm(vec[0], own[b])

    loads[1 + halves].wait()
    for i in range(parts):
        for j in range(parts):
            keep = shell_mask[i, 0, j].astype(F32)
            block = shell_raw[pl.ds(i * BLK, BLK), pl.ds(j * BLK, BLK)].astype(F32) * keep
            up[pl.ds(i * BLK, BLK), pl.ds(j * BLK, BLK)] = block.astype(BF16)

    @pl.when(has_up)
    def _():
        lift[0] = mm(vec[0], up[...]).astype(BF16)

    for h in range(halves):
        start_lift(0, h)

    loads[2 + halves].wait()

    def begin(step, part):
        v = vec[step, part]
        acc[step, part] = mm_t(v, local_raw[...]) + mm(v, local_raw[...]) - spectrum_center * v.astype(F32)

    begin(0, pl.ds(0, halves * LANES))

    for b in range(bits):
        @pl.when(holds[b])
        def _():
            block_copy(b).wait_recv()
            reply[0, b] = (partial[b] + mm_t(vec[0], theirs[b])).astype(BF16)
            reply_copy(0, b, 0).start()

        if b == 0:
            for c in range(bits):
                @pl.when(gives[c])
                def _():
                    block_copy(c).wait_send()
                    given_copy(0, c, 0).start()

    for h in range(1, halves):
        for b in range(bits):
            @pl.when(gives[b])
            def _():
                given_copy(0, b, h - 1).wait_send()
                given_copy(0, b, h).start()

            @pl.when(holds[b])
            def _():
                reply_copy(0, b, h - 1).wait_send()
                reply_copy(0, b, h).start()

    def gather(step, h):
        part = columns(h)

        @pl.when(has_up)
        def _():
            down_copy(step, h).wait_recv()
            acc[step, part] += mm_t(from_up[step, part], up[...])

        @pl.when(has_down)
        def _():
            rise_copy(step, h).wait_recv()
            acc[step, part] += from_down[step, part].astype(F32)

        for b in range(bits):
            @pl.when(holds[b])
            def _():
                given_copy(step, b, h).wait_recv()
                x = arrived[step, b, part]
                acc[step, part] += mm_t(x, own[b]) + mm(x, theirs[b])

        for b in range(bits):
            @pl.when(gives[b])
            def _():
                reply_copy(step, b, h).wait_recv()
                acc[step, part] += arrived[step, b, part].astype(F32)

    for h in range(halves):
        part = columns(h)
        gather(0, h)
        vec[1, part] = (acc[0, part] * (1.0 / spectrum_halfwidth)).astype(BF16)
        send_vectors(1, h)
        for b in order:
            @pl.when(holds[b])
            def _():
                v = vec[1, part]
                reply[1, b, part] = (mm(v, own[b]) + mm_t(v, theirs[b])).astype(BF16)
                reply_copy(1, b, h).start()

        @pl.when(has_up)
        def _():
            lift[1, part] = mm(vec[1, part], up[...]).astype(BF16)

        start_lift(1, h)
        begin(1, part)

    for h in range(halves):
        gather(1, h)
        for i in range(parts):
            here = pl.ds(i * BLK, BLK)
            y2 = (acc[1, columns(h), here] * (2.0 / spectrum_halfwidth)).T - vec_raw[here, columns(h)].astype(F32)
            out[here, columns(h)] = y2.astype(BF16)

    for b in range(bits):
        @pl.when(gives[b])
        def _():
            given_copy(0, b, halves - 1).wait_send()
            for h in range(halves):
                given_copy(1, b, h).wait_send()

        @pl.when(holds[b])
        def _():
            reply_copy(0, b, halves - 1).wait_send()
            for h in range(halves):
                reply_copy(1, b, h).wait_send()

    @pl.when(has_down)
    def _():
        for step in range(2):
            for h in range(halves):
                down_copy(step, h).wait_send()

    @pl.when(has_up)
    def _():
        for step in range(2):
            for h in range(halves):
                rise_copy(step, h).wait_send()


def on_device(bits, shells, vectors, local_block, pair_blocks, pair_masks, shell_block, shell_mask, matchings):
    rows, width = vectors.shape[2:]
    matches = pair_blocks.shape[2]
    halves = width // LANES
    parts = pair_masks.shape[-1]
    pair_masks = pair_masks.reshape(matches * parts, 1, parts)
    shell_mask = shell_mask.reshape(parts, 1, parts)
    square = (rows, rows)
    wide = (width, rows)
    out = pl.pallas_call(
        functools.partial(filter_kernel, bits, shells),
        out_shape=jax.ShapeDtypeStruct((rows, width), BF16),
        in_specs=[pl.BlockSpec(memory_space=pltpu.HBM)] * 7,
        out_specs=pl.BlockSpec(memory_space=pltpu.VMEM),
        scratch_shapes=[
            pltpu.SMEM(pair_masks.shape, jnp.int32),
            pltpu.SMEM(shell_mask.shape, jnp.int32),
            pltpu.SMEM(matchings.shape, jnp.int32),
            pltpu.VMEM((rows, width), BF16),
            pltpu.VMEM((2,) + wide, BF16),
            pltpu.VMEM(square, BF16),
            pltpu.VMEM((matches,) + square, BF16),
            pltpu.VMEM(square, BF16),
            pltpu.VMEM((bits,) + square, BF16),
            pltpu.VMEM((bits,) + square, BF16),
            pltpu.VMEM(square, BF16),
            pltpu.VMEM((bits,) + wide, F32),
            pltpu.VMEM((2, bits) + wide, BF16),
            pltpu.VMEM((2, bits) + wide, BF16),
            pltpu.VMEM((2,) + wide, BF16),
            pltpu.VMEM((2,) + wide, BF16),
            pltpu.VMEM((2,) + wide, BF16),
            pltpu.VMEM((2,) + wide, F32),
            pltpu.SemaphoreType.DMA((6 + halves,)),
            pltpu.SemaphoreType.DMA((bits,)),
            pltpu.SemaphoreType.DMA((bits,)),
            pltpu.SemaphoreType.DMA((2, bits, halves)),
            pltpu.SemaphoreType.DMA((2, bits, halves)),
            pltpu.SemaphoreType.DMA((2, halves)),
            pltpu.SemaphoreType.DMA((2, halves)),
            pltpu.SemaphoreType.DMA((2, halves)),
            pltpu.SemaphoreType.DMA((2, halves)),
        ],
        compiler_params=pltpu.CompilerParams(
            collective_id=0, has_side_effects=True, vmem_limit_bytes=40 * 1024 * 1024
        ),
    )(*[
        pltpu.with_memory_space_constraint(x, pltpu.HBM)
        for x in (
            vectors[0, 0],
            local_block[0, 0],
            pair_blocks[0, 0],
            shell_block[0, 0],
            pair_masks,
            shell_mask,
            matchings,
        )
    ])
    return out[None, None]


def solution(mesh):
    sizes = dict(mesh.shape)
    bits = sizes["grp"].bit_length() - 1
    in_specs = (
        P("grp", "shell", None, None),
        P("grp", "shell", None, None),
        P("grp", "shell", None, None, None),
        P("grp", "shell", None, None, None),
        P("grp", "shell", None, None),
        P("grp", "shell", None, None),
        P(),
    )
    out_specs = P("grp", "shell", None, None)
    return jax.shard_map(
        functools.partial(on_device, bits, sizes["shell"]),
        mesh=mesh, in_specs=in_specs, out_specs=out_specs, check_vma=False,
    )
```

```python
import functools

import jax
import jax.numpy as jnp
from jax import lax
from jax.experimental import pallas as pl
from jax.experimental.pallas import tpu as pltpu
from jax.sharding import PartitionSpec as P

BLK = 128
LANES = 128

spectrum_center = 1.0
spectrum_halfwidth = 6.0

MESH = pl.DeviceIdType.MESH
F32 = jnp.float32
BF16 = jnp.bfloat16


def mm(a, b):
    return jnp.dot(a, b, preferred_element_type=F32)


def mm_t(a, b):
    return lax.dot_general(a, b, (((1,), (1,)), ((), ())), preferred_element_type=F32)


def turned(x):
    return x.astype(F32).T


def filter_kernel(
    bits,
    shells,
    vec_hbm,
    local_hbm,
    pair_hbm,
    shell_hbm,
    pair_mask_hbm,
    shell_mask_hbm,
    matchings_hbm,
    out,
    pair_mask,
    shell_mask,
    matchings,
    vec_raw,
    vec,
    local_raw,
    pair_raw,
    shell_raw,
    own,
    theirs,
    up,
    partial,
    reply,
    arrived,
    lift,
    from_up,
    from_down,
    acc,
    load_sem,
    block_send,
    block_recv,
    edge_send,
    edge_recv,
    down_send,
    down_recv,
    rise_send,
    rise_recv,
):
    halves = vec.shape[1] // LANES
    rows = vec.shape[2]
    parts = rows // BLK
    matches = pair_raw.shape[0]
    group = lax.axis_index("grp")
    shell = lax.axis_index("shell")
    has_up = shell < shells - 1
    has_down = shell > 0
    order = list(reversed(range(bits)))

    def digit(b):
        return (group // (1 << b)) % 2

    partner = [group + (1 << b) - 2 * (1 << b) * digit(b) for b in range(bits)]
    other = [bits - 1] + [(b + 1) % bits for b in range(1, bits)]
    role = [(digit(b) + (digit(other[b]) if bits > 1 else 0) + (b == 0) + shell) % 2 for b in range(bits)]
    holds = [role[b] == 1 for b in range(bits)]
    gives = [role[b] == 0 for b in range(bits)]

    columns = lambda h: pl.ds(h * LANES, LANES)
    loads = [pltpu.make_async_copy(pair_hbm, pair_raw, load_sem.at[0])]
    for h in range(halves):
        loads.append(pltpu.make_async_copy(vec_hbm.at[:, columns(h)], vec_raw.at[:, columns(h)], load_sem.at[1 + h]))
    loads.append(pltpu.make_async_copy(shell_hbm, shell_raw, load_sem.at[1 + halves]))
    loads.append(pltpu.make_async_copy(local_hbm, local_raw, load_sem.at[2 + halves]))
    tables = [
        pltpu.make_async_copy(matchings_hbm, matchings, load_sem.at[3 + halves]),
        pltpu.make_async_copy(pair_mask_hbm, pair_mask, load_sem.at[4 + halves]),
        pltpu.make_async_copy(shell_mask_hbm, shell_mask, load_sem.at[5 + halves]),
    ]
    for load in tables + loads:
        load.start()

    def block_copy(b):
        return pltpu.make_async_remote_copy(
            src_ref=own.at[b], dst_ref=theirs.at[b], send_sem=block_send.at[b], recv_sem=block_recv.at[b],
            device_id={"grp": partner[b]}, device_id_type=MESH)

    def edge_copy(source, step, b, h):
        return pltpu.make_async_remote_copy(
            src_ref=source, dst_ref=arrived.at[step, b, columns(h)], send_sem=edge_send.at[step, b, h],
            recv_sem=edge_recv.at[step, b, h], device_id={"grp": partner[b]}, device_id_type=MESH)

    def given_copy(step, b, h):
        return edge_copy(vec.at[step, columns(h)], step, b, h)

    def reply_copy(step, b, h):
        return edge_copy(reply.at[step, b, columns(h)], step, b, h)

    def down_copy(step, h):
        return pltpu.make_async_remote_copy(
            src_ref=vec.at[step, columns(h)], dst_ref=from_up.at[step, columns(h)], send_sem=down_send.at[step, h],
            recv_sem=down_recv.at[step, h], device_id={"shell": shell - 1}, device_id_type=MESH)

    def rise_copy(step, h):
        return pltpu.make_async_remote_copy(
            src_ref=lift.at[step, columns(h)], dst_ref=from_down.at[step, columns(h)], send_sem=rise_send.at[step, h],
            recv_sem=rise_recv.at[step, h], device_id={"shell": shell + 1}, device_id_type=MESH)

    barrier = pltpu.get_barrier_semaphore()
    for b in range(bits):
        pl.semaphore_signal(barrier, inc=1, device_id={"grp": partner[b]}, device_id_type=MESH)

    @pl.when(has_up)
    def _():
        pl.semaphore_signal(barrier, inc=1, device_id={"shell": shell + 1}, device_id_type=MESH)

    @pl.when(has_down)
    def _():
        pl.semaphore_signal(barrier, inc=1, device_id={"shell": shell - 1}, device_id_type=MESH)

    neighbours = bits + jnp.where(has_up, 1, 0) + jnp.where(has_down, 1, 0)

    for table in tables:
        table.wait()
    flips = [jnp.bitwise_xor(matchings[m, group], group) for m in range(matches)]
    loads[0].wait()
    for at, b in enumerate(order):
        hits = [jnp.where(flips[m] == (1 << b), 1, 0) for m in range(matches)]
        which = jnp.minimum(sum(m * hits[m] for m in range(matches)), matches - 1)
        present = sum(hits)
        for i in range(parts):
            for j in range(parts):
                keep = (pair_mask[which * parts + i, 0, j] * present).astype(F32)
                block = pair_raw[which, pl.ds(i * BLK, BLK), pl.ds(j * BLK, BLK)]
                own[b, pl.ds(i * BLK, BLK), pl.ds(j * BLK, BLK)] = (block.astype(F32) * keep).astype(BF16)
        if at == 0:
            pl.semaphore_wait(barrier, neighbours)

        @pl.when(gives[b])
        def _():
            block_copy(b).start()

    def send_down(step, h):
        @pl.when(has_down)
        def _():
            down_copy(step, h).start()

    def send_vectors(step, h):
        for b in order:
            @pl.when(gives[b])
            def _():
                given_copy(step, b, h).start()

        send_down(step, h)

    def start_lift(step, h):
        @pl.when(has_up)
        def _():
            rise_copy(step, h).start()

    for h in range(halves):
        loads[1 + h].wait()
        for i in range(parts):
            here = pl.ds(i * BLK, BLK)
            vec[0, columns(h), here] = turned(vec_raw[here, columns(h)]).astype(BF16)
        if h == 0:
            send_vectors(0, h)
        else:
            send_down(0, h)

    for b in range(bits):
        @pl.when(holds[b])
        def _():
            partial[b] = mm(vec[0], own[b])

    loads[1 + halves].wait()
    for i in range(parts):
        for j in range(parts):
            keep = shell_mask[i, 0, j].astype(F32)
            block = shell_raw[pl.ds(i * BLK, BLK), pl.ds(j * BLK, BLK)].astype(F32) * keep
            up[pl.ds(i * BLK, BLK), pl.ds(j * BLK, BLK)] = block.astype(BF16)

    @pl.when(has_up)
    def _():
        lift[0] = mm(vec[0], up[...]).astype(BF16)

    for h in range(halves):
        start_lift(0, h)

    loads[2 + halves].wait()

    def begin(step, part):
        v = vec[step, part]
        acc[step, part] = mm_t(v, local_raw[...]) + mm(v, local_raw[...]) - spectrum_center * v.astype(F32)

    begin(0, pl.ds(0, halves * LANES))

    for b in range(bits):
        @pl.when(holds[b])
        def _():
            block_copy(b).wait_recv()
            reply[0, b] = (partial[b] + mm_t(vec[0], theirs[b])).astype(BF16)
            reply_copy(0, b, 0).start()

        if b == 0:
            for c in range(bits):
                @pl.when(gives[c])
                def _():
                    block_copy(c).wait_send()
                    for h in range(1, halves):
                        given_copy(0, c, h).start()

    for h in range(1, halves):
        for b in range(bits):
            @pl.when(holds[b])
            def _():
                reply_copy(0, b, h - 1).wait_send()
                reply_copy(0, b, h).start()

    def gather(step, h):
        part = columns(h)

        @pl.when(has_up)
        def _():
            down_copy(step, h).wait_recv()
            acc[step, part] += mm_t(from_up[step, part], up[...])

        @pl.when(has_down)
        def _():
            rise_copy(step, h).wait_recv()
            acc[step, part] += from_down[step, part].astype(F32)

        for b in range(bits):
            @pl.when(holds[b])
            def _():
                given_copy(step, b, h).wait_recv()
                x = arrived[step, b, part]
                acc[step, part] += mm_t(x, own[b]) + mm(x, theirs[b])

        for b in range(bits):
            @pl.when(gives[b])
            def _():
                reply_copy(step, b, h).wait_recv()
                acc[step, part] += arrived[step, b, part].astype(F32)

    for h in range(halves):
        part = columns(h)
        gather(0, h)
        vec[1, part] = (acc[0, part] * (1.0 / spectrum_halfwidth)).astype(BF16)
        send_vectors(1, h)
        for b in order:
            @pl.when(holds[b])
            def _():
                v = vec[1, part]
                reply[1, b, part] = (mm(v, own[b]) + mm_t(v, theirs[b])).astype(BF16)
                reply_copy(1, b, h).start()

        @pl.when(has_up)
        def _():
            lift[1, part] = mm(vec[1, part], up[...]).astype(BF16)

        start_lift(1, h)
        begin(1, part)

    for h in range(halves):
        gather(1, h)
        for i in range(parts):
            here = pl.ds(i * BLK, BLK)
            y2 = (acc[1, columns(h), here] * (2.0 / spectrum_halfwidth)).T - vec_raw[here, columns(h)].astype(F32)
            out[here, columns(h)] = y2.astype(BF16)

    for b in range(bits):
        @pl.when(gives[b])
        def _():
            for step in range(2):
                for h in range(halves):
                    given_copy(step, b, h).wait_send()

        @pl.when(holds[b])
        def _():
            reply_copy(0, b, halves - 1).wait_send()
            for h in range(halves):
                reply_copy(1, b, h).wait_send()

    @pl.when(has_down)
    def _():
        for step in range(2):
            for h in range(halves):
                down_copy(step, h).wait_send()

    @pl.when(has_up)
    def _():
        for step in range(2):
            for h in range(halves):
                rise_copy(step, h).wait_send()


def on_device(bits, shells, vectors, local_block, pair_blocks, pair_masks, shell_block, shell_mask, matchings):
    rows, width = vectors.shape[2:]
    matches = pair_blocks.shape[2]
    halves = width // LANES
    parts = pair_masks.shape[-1]
    pair_masks = pair_masks.reshape(matches * parts, 1, parts)
    shell_mask = shell_mask.reshape(parts, 1, parts)
    square = (rows, rows)
    wide = (width, rows)
    out = pl.pallas_call(
        functools.partial(filter_kernel, bits, shells),
        out_shape=jax.ShapeDtypeStruct((rows, width), BF16),
        in_specs=[pl.BlockSpec(memory_space=pltpu.HBM)] * 7,
        out_specs=pl.BlockSpec(memory_space=pltpu.VMEM),
        scratch_shapes=[
            pltpu.SMEM(pair_masks.shape, jnp.int32),
            pltpu.SMEM(shell_mask.shape, jnp.int32),
            pltpu.SMEM(matchings.shape, jnp.int32),
            pltpu.VMEM((rows, width), BF16),
            pltpu.VMEM((2,) + wide, BF16),
            pltpu.VMEM(square, BF16),
            pltpu.VMEM((matches,) + square, BF16),
            pltpu.VMEM(square, BF16),
            pltpu.VMEM((bits,) + square, BF16),
            pltpu.VMEM((bits,) + square, BF16),
            pltpu.VMEM(square, BF16),
            pltpu.VMEM((bits,) + wide, F32),
            pltpu.VMEM((2, bits) + wide, BF16),
            pltpu.VMEM((2, bits) + wide, BF16),
            pltpu.VMEM((2,) + wide, BF16),
            pltpu.VMEM((2,) + wide, BF16),
            pltpu.VMEM((2,) + wide, BF16),
            pltpu.VMEM((2,) + wide, F32),
            pltpu.SemaphoreType.DMA((6 + halves,)),
            pltpu.SemaphoreType.DMA((bits,)),
            pltpu.SemaphoreType.DMA((bits,)),
            pltpu.SemaphoreType.DMA((2, bits, halves)),
            pltpu.SemaphoreType.DMA((2, bits, halves)),
            pltpu.SemaphoreType.DMA((2, halves)),
            pltpu.SemaphoreType.DMA((2, halves)),
            pltpu.SemaphoreType.DMA((2, halves)),
            pltpu.SemaphoreType.DMA((2, halves)),
        ],
        compiler_params=pltpu.CompilerParams(
            collective_id=0, has_side_effects=True, vmem_limit_bytes=40 * 1024 * 1024
        ),
    )(*[
        pltpu.with_memory_space_constraint(x, pltpu.HBM)
        for x in (
            vectors[0, 0],
            local_block[0, 0],
            pair_blocks[0, 0],
            shell_block[0, 0],
            pair_masks,
            shell_mask,
            matchings,
        )
    ])
    return out[None, None]


def solution(mesh):
    sizes = dict(mesh.shape)
    bits = sizes["grp"].bit_length() - 1
    in_specs = (
        P("grp", "shell", None, None),
        P("grp", "shell", None, None),
        P("grp", "shell", None, None, None),
        P("grp", "shell", None, None, None),
        P("grp", "shell", None, None),
        P("grp", "shell", None, None),
        P(),
    )
    out_specs = P("grp", "shell", None, None)
    return jax.shard_map(
        functools.partial(on_device, bits, sizes["shell"]),
        mesh=mesh, in_specs=in_specs, out_specs=out_specs, check_vma=False,
    )
```

```python
import functools

import jax
import jax.numpy as jnp
from jax import lax
from jax.experimental import pallas as pl
from jax.experimental.pallas import tpu as pltpu
from jax.sharding import PartitionSpec as P

BLK = 128
LANES = 128

spectrum_center = 1.0
spectrum_halfwidth = 6.0

MESH = pl.DeviceIdType.MESH
F32 = jnp.float32
BF16 = jnp.bfloat16


def mm(a, b):
    return jnp.dot(a, b, preferred_element_type=F32)


def mm_t(a, b):
    return lax.dot_general(a, b, (((1,), (1,)), ((), ())), preferred_element_type=F32)


def turned(x):
    return x.astype(F32).T


def filter_kernel(
    bits,
    shells,
    vec_hbm,
    local_hbm,
    pair_hbm,
    shell_hbm,
    pair_mask_hbm,
    shell_mask_hbm,
    matchings_hbm,
    out,
    pair_mask,
    shell_mask,
    matchings,
    vec_raw,
    vec,
    local_raw,
    pair_raw,
    shell_raw,
    own,
    theirs,
    up,
    partial,
    reply,
    arrived,
    lift,
    from_up,
    from_down,
    acc,
    load_sem,
    block_send,
    block_recv,
    edge_send,
    edge_recv,
    down_send,
    down_recv,
    rise_send,
    rise_recv,
):
    halves = vec.shape[1] // LANES
    rows = vec.shape[2]
    parts = rows // BLK
    matches = pair_raw.shape[0]
    group = lax.axis_index("grp")
    shell = lax.axis_index("shell")
    has_up = shell < shells - 1
    has_down = shell > 0
    order = list(reversed(range(bits)))

    def digit(b):
        return (group // (1 << b)) % 2

    partner = [group + (1 << b) - 2 * (1 << b) * digit(b) for b in range(bits)]
    other = [bits - 1] + [(b + 1) % bits for b in range(1, bits)]
    role = [(digit(b) + (digit(other[b]) if bits > 1 else 0) + (b == 0) + shell) % 2 for b in range(bits)]
    holds = [role[b] == 1 for b in range(bits)]
    gives = [role[b] == 0 for b in range(bits)]

    columns = lambda h: pl.ds(h * LANES, LANES)
    loads = [pltpu.make_async_copy(pair_hbm, pair_raw, load_sem.at[0])]
    for h in range(halves):
        loads.append(pltpu.make_async_copy(vec_hbm.at[:, columns(h)], vec_raw.at[:, columns(h)], load_sem.at[1 + h]))
    loads.append(pltpu.make_async_copy(shell_hbm, shell_raw, load_sem.at[1 + halves]))
    loads.append(pltpu.make_async_copy(local_hbm, local_raw, load_sem.at[2 + halves]))
    tables = [
        pltpu.make_async_copy(matchings_hbm, matchings, load_sem.at[3 + halves]),
        pltpu.make_async_copy(pair_mask_hbm, pair_mask, load_sem.at[4 + halves]),
        pltpu.make_async_copy(shell_mask_hbm, shell_mask, load_sem.at[5 + halves]),
    ]
    for load in tables + loads:
        load.start()

    def block_copy(b):
        return pltpu.make_async_remote_copy(
            src_ref=own.at[b], dst_ref=theirs.at[b], send_sem=block_send.at[b], recv_sem=block_recv.at[b],
            device_id={"grp": partner[b]}, device_id_type=MESH)

    def edge_copy(source, step, b, h):
        return pltpu.make_async_remote_copy(
            src_ref=source, dst_ref=arrived.at[step, b, columns(h)], send_sem=edge_send.at[step, b, h],
            recv_sem=edge_recv.at[step, b, h], device_id={"grp": partner[b]}, device_id_type=MESH)

    def given_copy(step, b, h):
        return edge_copy(vec.at[step, columns(h)], step, b, h)

    def reply_copy(step, b, h):
        return edge_copy(reply.at[step, b, columns(h)], step, b, h)

    def down_copy(step, h):
        return pltpu.make_async_remote_copy(
            src_ref=vec.at[step, columns(h)], dst_ref=from_up.at[step, columns(h)], send_sem=down_send.at[step, h],
            recv_sem=down_recv.at[step, h], device_id={"shell": shell - 1}, device_id_type=MESH)

    def rise_copy(step, h):
        return pltpu.make_async_remote_copy(
            src_ref=lift.at[step, columns(h)], dst_ref=from_down.at[step, columns(h)], send_sem=rise_send.at[step, h],
            recv_sem=rise_recv.at[step, h], device_id={"shell": shell + 1}, device_id_type=MESH)

    barrier = pltpu.get_barrier_semaphore()
    for b in range(bits):
        pl.semaphore_signal(barrier, inc=1, device_id={"grp": partner[b]}, device_id_type=MESH)

    @pl.when(has_up)
    def _():
        pl.semaphore_signal(barrier, inc=1, device_id={"shell": shell + 1}, device_id_type=MESH)

    @pl.when(has_down)
    def _():
        pl.semaphore_signal(barrier, inc=1, device_id={"shell": shell - 1}, device_id_type=MESH)

    neighbours = bits + jnp.where(has_up, 1, 0) + jnp.where(has_down, 1, 0)

    for table in tables:
        table.wait()
    flips = [jnp.bitwise_xor(matchings[m, group], group) for m in range(matches)]
    loads[0].wait()
    for at, b in enumerate(order):
        hits = [jnp.where(flips[m] == (1 << b), 1, 0) for m in range(matches)]
        which = jnp.minimum(sum(m * hits[m] for m in range(matches)), matches - 1)
        present = sum(hits)
        for i in range(parts):
            for j in range(parts):
                keep = (pair_mask[which * parts + i, 0, j] * present).astype(F32)
                block = pair_raw[which, pl.ds(i * BLK, BLK), pl.ds(j * BLK, BLK)]
                own[b, pl.ds(i * BLK, BLK), pl.ds(j * BLK, BLK)] = (block.astype(F32) * keep).astype(BF16)
        if at == 0:
            pl.semaphore_wait(barrier, neighbours)

        @pl.when(gives[b])
        def _():
            block_copy(b).start()

    def send_vectors(step, h):
        for b in order:
            @pl.when(gives[b])
            def _():
                given_copy(step, b, h).start()

        @pl.when(has_down)
        def _():
            down_copy(step, h).start()

    def start_lift(step, h):
        @pl.when(has_up)
        def _():
            rise_copy(step, h).start()

    for h in range(halves):
        loads[1 + h].wait()
        for i in range(parts):
            here = pl.ds(i * BLK, BLK)
            vec[0, columns(h), here] = turned(vec_raw[here, columns(h)]).astype(BF16)
        send_vectors(0, h)

    for b in range(bits):
        @pl.when(holds[b])
        def _():
            partial[b] = mm(vec[0], own[b])

    loads[1 + halves].wait()
    for i in range(parts):
        for j in range(parts):
            keep = shell_mask[i, 0, j].astype(F32)
            block = shell_raw[pl.ds(i * BLK, BLK), pl.ds(j * BLK, BLK)].astype(F32) * keep
            up[pl.ds(i * BLK, BLK), pl.ds(j * BLK, BLK)] = block.astype(BF16)

    @pl.when(has_up)
    def _():
        lift[0] = mm(vec[0], up[...]).astype(BF16)

    for h in range(halves):
        start_lift(0, h)

    loads[2 + halves].wait()

    def begin(step, part):
        v = vec[step, part]
        acc[step, part] = mm_t(v, local_raw[...]) + mm(v, local_raw[...]) - spectrum_center * v.astype(F32)

    begin(0, pl.ds(0, halves * LANES))

    for b in range(bits):
        @pl.when(holds[b])
        def _():
            block_copy(b).wait_recv()
            reply[0, b] = (partial[b] + mm_t(vec[0], theirs[b])).astype(BF16)
            for h in range(halves):
                reply_copy(0, b, h).start()

    def gather(step, h):
        part = columns(h)

        @pl.when(has_up)
        def _():
            down_copy(step, h).wait_recv()
            acc[step, part] += mm_t(from_up[step, part], up[...])

        @pl.when(has_down)
        def _():
            rise_copy(step, h).wait_recv()
            acc[step, part] += from_down[step, part].astype(F32)

        for b in range(bits):
            @pl.when(holds[b])
            def _():
                given_copy(step, b, h).wait_recv()
                x = arrived[step, b, part]
                acc[step, part] += mm_t(x, own[b]) + mm(x, theirs[b])

        for b in range(bits):
            @pl.when(gives[b])
            def _():
                reply_copy(step, b, h).wait_recv()
                acc[step, part] += arrived[step, b, part].astype(F32)

    for h in range(halves):
        part = columns(h)
        gather(0, h)
        vec[1, part] = (acc[0, part] * (1.0 / spectrum_halfwidth)).astype(BF16)
        send_vectors(1, h)
        for b in order:
            @pl.when(holds[b])
            def _():
                v = vec[1, part]
                reply[1, b, part] = (mm(v, own[b]) + mm_t(v, theirs[b])).astype(BF16)
                reply_copy(1, b, h).start()

        @pl.when(has_up)
        def _():
            lift[1, part] = mm(vec[1, part], up[...]).astype(BF16)

        start_lift(1, h)
        begin(1, part)

    for h in range(halves):
        gather(1, h)
        for i in range(parts):
            here = pl.ds(i * BLK, BLK)
            y2 = (acc[1, columns(h), here] * (2.0 / spectrum_halfwidth)).T - vec_raw[here, columns(h)].astype(F32)
            out[here, columns(h)] = y2.astype(BF16)

    for b in range(bits):
        @pl.when(gives[b])
        def _():
            block_copy(b).wait_send()
            for step in range(2):
                for h in range(halves):
                    given_copy(step, b, h).wait_send()

        @pl.when(holds[b])
        def _():
            for step in range(2):
                for h in range(halves):
                    reply_copy(step, b, h).wait_send()

    @pl.when(has_down)
    def _():
        for step in range(2):
            for h in range(halves):
                down_copy(step, h).wait_send()

    @pl.when(has_up)
    def _():
        for step in range(2):
            for h in range(halves):
                rise_copy(step, h).wait_send()


def on_device(bits, shells, vectors, local_block, pair_blocks, pair_masks, shell_block, shell_mask, matchings):
    rows, width = vectors.shape[2:]
    matches = pair_blocks.shape[2]
    halves = width // LANES
    parts = pair_masks.shape[-1]
    pair_masks = pair_masks.reshape(matches * parts, 1, parts)
    shell_mask = shell_mask.reshape(parts, 1, parts)
    square = (rows, rows)
    wide = (width, rows)
    out = pl.pallas_call(
        functools.partial(filter_kernel, bits, shells),
        out_shape=jax.ShapeDtypeStruct((rows, width), BF16),
        in_specs=[pl.BlockSpec(memory_space=pltpu.HBM)] * 7,
        out_specs=pl.BlockSpec(memory_space=pltpu.VMEM),
        scratch_shapes=[
            pltpu.SMEM(pair_masks.shape, jnp.int32),
            pltpu.SMEM(shell_mask.shape, jnp.int32),
            pltpu.SMEM(matchings.shape, jnp.int32),
            pltpu.VMEM((rows, width), BF16),
            pltpu.VMEM((2,) + wide, BF16),
            pltpu.VMEM(square, BF16),
            pltpu.VMEM((matches,) + square, BF16),
            pltpu.VMEM(square, BF16),
            pltpu.VMEM((bits,) + square, BF16),
            pltpu.VMEM((bits,) + square, BF16),
            pltpu.VMEM(square, BF16),
            pltpu.VMEM((bits,) + wide, F32),
            pltpu.VMEM((2, bits) + wide, BF16),
            pltpu.VMEM((2, bits) + wide, BF16),
            pltpu.VMEM((2,) + wide, BF16),
            pltpu.VMEM((2,) + wide, BF16),
            pltpu.VMEM((2,) + wide, BF16),
            pltpu.VMEM((2,) + wide, F32),
            pltpu.SemaphoreType.DMA((6 + halves,)),
            pltpu.SemaphoreType.DMA((bits,)),
            pltpu.SemaphoreType.DMA((bits,)),
            pltpu.SemaphoreType.DMA((2, bits, halves)),
            pltpu.SemaphoreType.DMA((2, bits, halves)),
            pltpu.SemaphoreType.DMA((2, halves)),
            pltpu.SemaphoreType.DMA((2, halves)),
            pltpu.SemaphoreType.DMA((2, halves)),
            pltpu.SemaphoreType.DMA((2, halves)),
        ],
        compiler_params=pltpu.CompilerParams(
            collective_id=0, has_side_effects=True, vmem_limit_bytes=40 * 1024 * 1024
        ),
    )(*[
        pltpu.with_memory_space_constraint(x, pltpu.HBM)
        for x in (
            vectors[0, 0],
            local_block[0, 0],
            pair_blocks[0, 0],
            shell_block[0, 0],
            pair_masks,
            shell_mask,
            matchings,
        )
    ])
    return out[None, None]


def solution(mesh):
    sizes = dict(mesh.shape)
    bits = sizes["grp"].bit_length() - 1
    in_specs = (
        P("grp", "shell", None, None),
        P("grp", "shell", None, None),
        P("grp", "shell", None, None, None),
        P("grp", "shell", None, None, None),
        P("grp", "shell", None, None),
        P("grp", "shell", None, None),
        P(),
    )
    out_specs = P("grp", "shell", None, None)
    return jax.shard_map(
        functools.partial(on_device, bits, sizes["shell"]),
        mesh=mesh, in_specs=in_specs, out_specs=out_specs, check_vma=False,
    )
```
